128 devices in a mesh: dp: 4 (over y_lo, core), mp: 32 (over z, y_hi, x).
Axes of the slice: x: 4, y: 4 (y_hi: 2, y_lo: 2; y = y_hi * 2 + y_lo), z: 4, core: 2. Of those that a mesh axis runs over, the one named last changes fastest.
Arguments:
- hidden_states: bfloat16 [4096, 16384], P('dp', 'mp'), may hold values from -400 to 400, as said below
- norm_gain: bfloat16 [16384], P('mp'), may hold values from 0.5 to 1.5
- damping: float32 [16384], P('mp'), may hold values from 0.05 to 0.5
Outputs:
- hessian: float32 [2048, 16384], P('dp', 'mp')
- factor_rows: float32 [1024, 16384], P('dp', 'mp')
- updated_rows: float32 [1024, 16384], P('dp', 'mp')
The draws below stay inside these ranges and needn't reach their ends.
Inputs may be any that keep to these rules, and one draw needn't show every extreme that they name: `hidden_states`: activations with token scales and feature scales of different sizes.
All inputs are finite; a program needn't handle non-finite values.
Results may differ from the reference program's by a relative error of at most 0.0038.
Values may be sent and summed in bfloat16 or wider, within the bound.
A program may use at most 128 MiB of HBM per device.

```python
import math
import jax
import jax.numpy as jnp
from jax import lax

D = 16384
PANEL = 1024
TOKENS = 4096


def draw_hidden_states(key, part):
    key = jax.random.fold_in(key, 7)
    key_base, key_rows, key_cols = jax.random.split(key, 3)
    position = jnp.arange(D, dtype=jnp.float32) / D
    col_scale = jnp.exp(jnp.log(3.0) * position + jax.random.uniform(key_cols, (D,), jnp.float32, 0.0, jnp.log(10.0 / 3.0)))
    base_values = jnp.clip(jax.random.normal(key_base, (TOKENS, D), jnp.float32), -4.0, 4.0)
    row_scale = jnp.exp(jax.random.uniform(key_rows, (TOKENS, 1), jnp.float32, 0.0, jnp.log(10.0)))
    return (base_values * row_scale * col_scale[None, :]).astype(jnp.bfloat16)


def block_scale(rng, shape, cuts, smallest, high):
    loudness = 1.0
    for axis_at, parts in cuts:
        heights = jax.random.uniform(jax.random.fold_in(jax.random.fold_in(rng, 6), axis_at), (parts,), jnp.float32, smallest / len(cuts), high / len(cuts))
        loudness = loudness * jnp.repeat(jnp.exp(heights), shape[axis_at] // parts).reshape((-1,) + (1,) * (len(shape) - 1 - axis_at))
    return loudness


def setup_inputs(seed: int = 0) -> dict:
    arg_keys = jax.random.split(jax.random.key(seed), 4)
    return {
        "hidden_states": draw_hidden_states(jax.random.fold_in(arg_keys[3], 71), 0),
        "norm_gain": jnp.clip(1.0 + 0.1 * jax.random.normal(arg_keys[1], (D,), jnp.float32), 0.5, 1.5).astype(jnp.bfloat16),
        "damping": jnp.clip(jnp.exp(math.log(0.5) - 2.3025851 * jax.random.uniform(arg_keys[2], (D,), jnp.float32) ** block_scale(arg_keys[2], (D,), ((0, 32),), -0.2, 0.2)), 0.05, 0.5),
    }


def reference(hidden_states, norm_gain, damping):
    span_rows = 2 * PANEL
    values = hidden_states.astype(jnp.float32)
    ssq = lax.optimization_barrier(jnp.sum(values * values, axis=1))
    inverse_rms = lax.rsqrt(ssq / D + 1e-05)
    normed = (values * inverse_rms[:, None] * norm_gain.astype(jnp.float32)[None, :]).astype(jnp.bfloat16)
    widened = normed.astype(jnp.float32)
    gram_window = jnp.dot(widened[:, :span_rows].T, widened, precision=lax.Precision.HIGHEST) / TOKENS
    diag_index = jnp.arange(span_rows, dtype=jnp.int32)
    hessian = gram_window.at[diag_index, diag_index].add(damping[:span_rows])
    lower_factor = jnp.linalg.cholesky(hessian[:PANEL, :PANEL])
    upper_rows = lax.linalg.triangular_solve(lower_factor, hessian[:PANEL], left_side=True, lower=True)
    updated_rows = hessian[PANEL:] - jnp.dot(upper_rows[:, PANEL:span_rows].T, upper_rows, precision=lax.Precision.HIGHEST)
    return (hessian, upper_rows, updated_rows)
```

```python
import functools

import jax
import jax.numpy as jnp
from jax import lax
from jax.experimental import pallas as pl
from jax.experimental.pallas import tpu as pltpu
from jax.sharding import PartitionSpec as P

D = 16384
PANEL = 1024
TOKENS = 4096
MESH = pl.DeviceIdType.MESH
HI = lax.Precision.HIGHEST
F32 = jnp.float32
VM = pl.BlockSpec(memory_space=pltpu.VMEM)


def params(**kw):
    return pltpu.CompilerParams(vmem_limit_bytes=56 * 2**20, **kw)


def spot():
    mp = lax.axis_index("mp")
    return lax.axis_index("dp"), mp // 8, (mp // 4) % 2, mp % 4


def at(dp, z, h, x):
    return (dp, z * 8 + h * 4 + x)


def greet(partners):
    barrier = pltpu.get_barrier_semaphore()
    for p in partners:
        pl.semaphore_signal(barrier, inc=1, device_id=p, device_id_type=MESH)
    pl.semaphore_wait(barrier, len(partners))


def spread_kernel(x_ref, aux_ref, w_ref, auxs_ref, ssq_ref, sx, sz, sh, s0s, s0r, ps, pr, qs, qr):
    dp, z, h, x = spot()
    column = [at(dp, (z + q // 2) % 4, (h + q % 2) % 2, x) for q in range(1, 8)]
    ring_x = [at(dp, z, h, (x + j) % 4) for j in range(1, 4)]
    ring_z = [at(dp, (z + j) % 4, h, x) for j in range(1, 4)]
    peer_h = at(dp, z, 1 - h, x)
    greet(column + ring_x)

    def copy(src, dst, ss, rs, dev):
        return pltpu.make_async_remote_copy(src_ref=src, dst_ref=dst, send_sem=ss, recv_sem=rs,
                                            device_id=dev, device_id_type=MESH)

    def rows_of(zz, hh):
        return pl.multiple_of(zz * 128 + hh * 64, 64)

    is_source = (z == 0) & (h == 0)

    def scatter(q):
        a = (q // 2) * 128 + (q % 2) * 64
        return [
            copy(aux_ref, auxs_ref.at[x], s0s.at[3 * q + 2], s0r.at[2], column[q - 1]),
            copy(x_ref.at[pl.ds(a, 64)], w_ref.at[x, pl.ds(a, 64)], s0s.at[3 * q], s0r.at[0], column[q - 1]),
            copy(x_ref.at[pl.ds(512 + a, 64)], w_ref.at[x, pl.ds(512 + a, 64)], s0s.at[3 * q + 1], s0r.at[1],
                 column[q - 1]),
        ]

    @pl.when(is_source)
    def _():
        for q in range(1, 8):
            for c in scatter(q):
                c.start()
        w_ref[x, 0:64] = x_ref[0:64]
        w_ref[x, 512:576] = x_ref[512:576]
        auxs_ref[x] = aux_ref[...]

    part = jnp.zeros((1024, 128), F32)
    for i in range(4):
        v = x_ref[:, 128 * i:128 * i + 128].astype(F32)
        part = part + v * v
    line = jnp.sum(part.T, axis=0, keepdims=True)
    for i in range(8):
        sx[x, i:i + 1, :] = line[:, 128 * i:128 * i + 128]
    sum_x = [copy(sx.at[x], sx.at[x], qs.at[j], qr.at[j], ring_x[j]) for j in range(3)]
    for c in sum_x:
        c.start()

    @pl.when(jnp.logical_not(is_source))
    def _():
        for c in scatter(1):
            c.wait_recv()

    own = rows_of(z, h)
    pair = pl.multiple_of(z * 128, 128)
    half_a = w_ref.at[x, pl.ds(own, 64)]
    half_b = w_ref.at[x, pl.ds(512 + own, 64)]
    step_h = [copy(half_a, half_a, ps.at[0], pr.at[0], peer_h), copy(half_b, half_b, ps.at[1], pr.at[1], peer_h)]
    for c in step_h:
        c.start()
    step_aux = [copy(auxs_ref.at[x], auxs_ref.at[x], ps.at[2 + j], pr.at[2 + j], ring_x[j]) for j in range(3)]
    for c in step_aux:
        c.start()
    for c in sum_x:
        c.wait_recv()
    sz[z] = (sx[0] + sx[1]) + (sx[2] + sx[3])
    sum_z = [copy(sz.at[z], sz.at[z], qs.at[3 + j], qr.at[3 + j], ring_z[j]) for j in range(3)]
    for c in sum_z:
        c.start()

    both_a = w_ref.at[x, pl.ds(pair, 128)]
    both_b = w_ref.at[x, pl.ds(512 + pair, 128)]
    step_2a = [copy(both_a, both_a, ps.at[5 + j], pr.at[5 + j], ring_x[j]) for j in range(3)]
    step_2b = [copy(both_b, both_b, ps.at[8 + j], pr.at[8 + j], ring_z[j]) for j in range(3)]
    step_h[0].wait_recv()
    for c in step_2a:
        c.start()
    step_h[1].wait_recv()
    for c in step_2b:
        c.start()

    for c in sum_z:
        c.wait_recv()
    sh[h] = (sz[0] + sz[1]) + (sz[2] + sz[3])
    sum_h = copy(sh.at[h], sh.at[h], qs.at[6], qr.at[6], peer_h)
    sum_h.start()

    all_a = w_ref.at[:, pl.ds(pair, 128)]
    all_b = w_ref.at[x, pl.ds(512, 512)]
    step_3a = [copy(all_a, all_a, ps.at[11 + j], pr.at[11 + j], ring_z[j]) for j in range(3)]
    step_3b = [copy(all_b, all_b, ps.at[14 + j], pr.at[14 + j], ring_x[j]) for j in range(3)]
    for c in step_2a:
        c.wait_recv()
    for c in step_3a:
        c.start()
    for c in step_2b:
        c.wait_recv()
    for c in step_3b:
        c.start()
    sum_h.wait_recv()
    ssq_ref[...] = sh[0] + sh[1]
    for c in step_aux + step_3a + step_3b:
        c.wait_recv()
    for c in sum_x + sum_z + [sum_h] + step_h + step_aux + step_2a + step_2b + step_3a + step_3b:
        c.wait_send()

    @pl.when(is_source)
    def _():
        for q in range(1, 8):
            for c in scatter(q):
                c.wait_send()


def spread(hidden, aux):
    return pl.pallas_call(
        spread_kernel,
        out_shape=(
            jax.ShapeDtypeStruct((4, 1024, 512), jnp.bfloat16),
            jax.ShapeDtypeStruct((4, 8, 512), F32),
            jax.ShapeDtypeStruct((8, 128), F32),
        ),
        in_specs=[VM, VM],
        out_specs=(VM, VM, VM),
        scratch_shapes=[
            pltpu.VMEM((4, 8, 128), F32),
            pltpu.VMEM((4, 8, 128), F32),
            pltpu.VMEM((2, 8, 128), F32),
            pltpu.SemaphoreType.DMA((24,)),
            pltpu.SemaphoreType.DMA((3,)),
            pltpu.SemaphoreType.DMA((17,)),
            pltpu.SemaphoreType.DMA((17,)),
            pltpu.SemaphoreType.DMA((7,)),
            pltpu.SemaphoreType.DMA((7,)),
        ],
        compiler_params=params(collective_id=0, has_side_effects=True),
        name="spread_window",
    )(hidden, aux)


def dot_t(a, b, precision=None):
    return lax.dot_general(a, b, (((0,), (0,)), ((), ())), precision=precision, preferred_element_type=F32)


def dot(a, b):
    return jnp.dot(a, b, precision=HI, preferred_element_type=F32)


def gram_kernel(w_ref, auxs_ref, ssq_ref, x_ref, aux_ref, slab_ref, share_ref, wn, xn, rms, wide):
    _, z, _, x = spot()
    inverse = lax.rsqrt(ssq_ref[...] / D + 1e-05)
    for i in range(8):
        rms[128 * i:128 * i + 128, :] = jnp.broadcast_to(inverse[i:i + 1, :], (128, 128)).T

    @pl.loop(0, 8)
    def _(i):
        rows = pl.ds(pl.multiple_of(i * 128, 128), 128)
        scale = jnp.concatenate([rms[rows, :]] * 4, axis=1)
        xn[rows, :] = (x_ref[rows, :].astype(F32) * scale * aux_ref[0:1, :]).astype(jnp.bfloat16)
        for b in range(4):
            wn[b, rows, :] = (w_ref[b, rows, :].astype(F32) * scale * auxs_ref[b, 0:1, :]).astype(jnp.bfloat16)

    s = z * 4 + x
    strip = wn[s // 8, :, pl.ds(pl.multiple_of(((s % 8) // 2) * 128, 128), 128)]
    for b in range(4):
        wide[:, 512 * b:512 * b + 512] = dot_t(strip, wn[b]) * (1.0 / TOKENS)
    share_ref[...] = wide[pl.ds(pl.multiple_of((s % 2) * 64, 64), 64), :]

    @pl.loop(0, 16)
    def _(i):
        left = wn[i // 4, :, pl.ds(pl.multiple_of((i % 4) * 128, 128), 128)]
        slab_ref[pl.ds(pl.multiple_of(i * 128, 128), 128), :] = dot_t(left, xn[...]) * (1.0 / TOKENS)


def gram(w, auxs, ssq, hidden, aux):
    return pl.pallas_call(
        gram_kernel,
        out_shape=(jax.ShapeDtypeStruct((2048, 512), F32), jax.ShapeDtypeStruct((64, 2048), F32)),
        in_specs=[VM] * 5,
        out_specs=(VM, VM),
        scratch_shapes=[
            pltpu.VMEM((4, 1024, 512), jnp.bfloat16),
            pltpu.VMEM((1024, 512), jnp.bfloat16),
            pltpu.VMEM((1024, 128), F32),
            pltpu.VMEM((128, 2048), F32),
        ],
        compiler_params=params(),
        name="partial_gram",
    )(w, auxs, ssq, hidden, aux)


def join_kernel(slab_ref, share_ref, g_ref, p_ref, other, share_in, share_sum, share_y, ss, rs):
    dp, z, h, x = spot()
    c, y = dp % 2, dp // 2
    peer_c = at(y * 2 + 1 - c, z, h, x)
    peer_y = at((1 - y) * 2 + c, z, h, x)
    ring_x = [at(dp, z, h, (x + j) % 4) for j in range(1, 4)]
    ring_z = [at(dp, (z + j) % 4, h, x) for j in range(1, 4)]
    greet([peer_c, peer_y] + ring_x + ring_z)

    def copy(src, dst, i, dev):
        return pltpu.make_async_remote_copy(src_ref=src, dst_ref=dst, send_sem=ss.at[i], recv_sem=rs.at[i],
                                            device_id=dev, device_id_type=MESH)

    to_core = copy(share_ref.at[pl.ds(pl.multiple_of(32 * (1 - c), 32), 32)], share_in, 0, peer_c)
    to_core.start()
    spans = [(512 * (1 - c), 0, 512), (1024 + 256 * (1 - c), 512, 256), (1536 + 256 * (1 - c), 768, 256)]
    slabs = [
        copy(slab_ref.at[pl.ds(pl.multiple_of(a, 256), n)], other.at[pl.ds(b, n)], 1 + i, peer_c)
        for i, (a, b, n) in enumerate(spans)
    ]
    to_core.wait_recv()
    share_sum[...] = share_ref[pl.ds(pl.multiple_of(32 * c, 32), 32), :] + share_in[...]
    give = pl.ds(pl.multiple_of(1024 + 512 * (1 - y), 512), 512)
    keep = pl.ds(pl.multiple_of(1024 + 512 * y, 512), 512)
    to_y = [
        copy(share_sum.at[:, pl.ds(0, 1024)], share_y.at[:, pl.ds(0, 1024)], 4, peer_y),
        copy(share_sum.at[:, give], share_y.at[:, pl.ds(1024, 512)], 5, peer_y),
    ]
    for k in to_y:
        k.start()
    for k in slabs:
        k.start()
    for k in to_y:
        k.wait_recv()
    g_ref[z, x, c, :, 0:1024] = share_sum[:, 0:1024] + share_y[:, 0:1024]
    g_ref[z, x, c, :, 1024:1536] = share_sum[:, keep] + share_y[:, 1024:1536]

    first, second = pl.ds(0, 16), pl.ds(16, 16)
    one_a, one_b = g_ref.at[z, x, c, first], g_ref.at[z, x, c, second]
    step_1a = [copy(one_a, one_a, 6 + j, ring_x[j]) for j in range(3)]
    step_1b = [copy(one_b, one_b, 9 + j, ring_z[j]) for j in range(3)]
    for k in step_1a + step_1b:
        k.start()
    row_a, row_b = g_ref.at[z, :, c, first], g_ref.at[:, x, c, second]
    step_2a = [copy(row_a, row_a, 12 + j, ring_z[j]) for j in range(3)]
    step_2b = [copy(row_b, row_b, 15 + j, ring_x[j]) for j in range(3)]
    for k in step_1a:
        k.wait_recv()
    for k in step_2a:
        k.start()
    for k in step_1b:
        k.wait_recv()
    for k in step_2b:
        k.start()
    for k in slabs:
        k.wait_recv()
    p_ref[0:512, :] = slab_ref[pl.ds(pl.multiple_of(512 * c, 512), 512), :] + other[0:512, :]
    p_ref[512:768, :] = slab_ref[pl.ds(pl.multiple_of(1024 + 256 * c, 256), 256), :] + other[512:768, :]
    p_ref[768:1024, :] = slab_ref[pl.ds(pl.multiple_of(1536 + 256 * c, 256), 256), :] + other[768:1024, :]
    for k in step_2a:
        k.wait_recv()
    full_a, full_b = g_ref.at[:, :, c, first], g_ref.at[:, :, c, second]
    last_a = copy(full_a, full_a, 18, peer_c)
    last_a.start()
    for k in step_2b:
        k.wait_recv()
    last_b = copy(full_b, full_b, 19, peer_c)
    last_b.start()
    last_a.wait_recv()
    last_b.wait_recv()
    for k in [to_core] + slabs + to_y + step_1a + step_1b + step_2a + step_2b + [last_a, last_b]:
        k.wait_send()


def join(slab, share):
    return pl.pallas_call(
        join_kernel,
        out_shape=(jax.ShapeDtypeStruct((4, 4, 2, 32, 1536), F32), jax.ShapeDtypeStruct((1024, 512), F32)),
        in_specs=[VM, VM],
        out_specs=(VM, VM),
        scratch_shapes=[
            pltpu.VMEM((1024, 512), F32),
            pltpu.VMEM((32, 2048), F32),
            pltpu.VMEM((32, 2048), F32),
            pltpu.VMEM((32, 1536), F32),
            pltpu.SemaphoreType.DMA((20,)),
            pltpu.SemaphoreType.DMA((20,)),
        ],
        compiler_params=params(collective_id=1, has_side_effects=True),
        name="join_window",
    )(slab, share)


def lane_of(v, j):
    return jnp.broadcast_to(v[:, j:j + 1], (8, 128))


def row_of(v, r):
    return jnp.broadcast_to(v[r:r + 1, :], (8, 128))


def factor_block(groups, lane, sub):
    done = [None] * 16
    groups = list(groups)
    for p in range(16):
        base = 8 * p
        here = groups[p]
        inside = (lane >= base) & (lane < base + 8)
        cols = [lane_of(here, base + t) for t in range(8)]
        a = {(r, t): row_of(cols[t], r) for t in range(8) for r in range(t + 1)}
        opened = jnp.where(inside, jnp.where(lane - base == sub, 1.0, 0.0), here)
        rows = [row_of(opened, r) for r in range(8)]
        has_next = p + 1 < 16
        if has_next:
            next_cols = [lane_of(groups[p + 1], base + t) for t in range(8)]
            next_group = jnp.where(inside, 0.0, groups[p + 1])
        m, inv = {}, {}
        out = jnp.zeros((8, 128), F32)
        for s in range(8):
            inv[s] = 1.0 / a[s, s]
            out = jnp.where(sub == s, rows[s] * lax.rsqrt(a[s, s]), out)
            for t in range(s + 1, 8):
                m[s, t] = a[s, t] * inv[s]
                for u in range(t, 8):
                    a[t, u] = a[t, u] - m[s, t] * a[s, u]
            if has_next:
                next_group = next_group - (next_cols[s] * inv[s]) * rows[s]
            for t in range(s + 1, 8):
                rows[t] = rows[t] - m[s, t] * rows[s]
                if has_next:
                    next_cols[t] = next_cols[t] - m[s, t] * next_cols[s]
        done[p] = out
        if p + 2 < 16:
            back = [None] * 8
            for s in range(7, -1, -1):
                g = rows[s] * inv[s]
                for t in range(s + 1, 8):
                    g = g - m[s, t] * back[t]
                back[s] = g
            for i in range(p + 2, 16):
                v = jnp.where(inside, 0.0, groups[i])
                for t in range(8):
                    v = v - lane_of(groups[i], base + t) * back[t]
                groups[i] = v
        if has_next:
            groups[p + 1] = next_group
    return jnp.concatenate(done, axis=0)


def factor_kernel(g_ref, auxs_ref, inv_ref, a_ref):
    lane = lax.broadcasted_iota(jnp.int32, (8, 128), 1)
    sub = lax.broadcasted_iota(jnp.int32, (8, 128), 0)
    row = lax.broadcasted_iota(jnp.int32, (128, 128), 0)
    col = lax.broadcasted_iota(jnp.int32, (128, 128), 1)
    n, blocks = PANEL, PANEL // 128
    a_ref[...] = g_ref[:, 0:PANEL]
    for k in range(blocks):
        at_k = slice(128 * k, 128 * k + 128)
        damp = auxs_ref[k // 4, 1:2, 128 * (k % 4):128 * (k % 4) + 128]
        a_ref[at_k, at_k] = a_ref[at_k, at_k] + jnp.where(row == col, damp, 0.0)
    for k in range(blocks):
        kb = 128 * k
        groups = [a_ref[kb + 8 * i:kb + 8 * i + 8, kb:kb + 128] for i in range(16)]
        inverse = jnp.where(row >= col, factor_block(groups, lane, sub), 0.0)
        inv_ref[kb:kb + 128, kb:kb + 128] = inverse
        if kb + 128 < n:
            inv_ref[kb:kb + 128, kb + 128:n] = jnp.zeros((128, n - kb - 128), F32)
            upper = dot(inverse, a_ref[kb:kb + 128, kb + 128:n])
        if k:
            left = dot(inverse, a_ref[kb:kb + 128, :kb])
            inv_ref[kb:kb + 128, :kb] = left
        for i in range(k + 1, blocks):
            ib = 128 * i
            mine = upper[:, ib - kb - 128:ib - kb]
            a_ref[ib:ib + 128, ib:n] = a_ref[ib:ib + 128, ib:n] - dot_t(mine, upper[:, ib - kb - 128:], HI)
            if k:
                a_ref[ib:ib + 128, :kb] = a_ref[ib:ib + 128, :kb] - dot_t(mine, left, HI)
            a_ref[ib:ib + 128, kb:kb + 128] = -dot_t(mine, inverse, HI)


def factor(g, auxs):
    return pl.pallas_call(
        factor_kernel,
        out_shape=jax.ShapeDtypeStruct((PANEL, PANEL), F32),
        in_specs=[VM, VM],
        out_specs=VM,
        scratch_shapes=[pltpu.VMEM((PANEL, PANEL), F32)],
        compiler_params=params(),
        cost_estimate=pl.CostEstimate(flops=20 * 10**9, bytes_accessed=200 * 2**20, transcendentals=0),
        name="panel_factor",
    )(g, auxs)


def finish_kernel(inv_ref, g_ref, f_ref, e_ref, aux_ref, hess_ref, fac_ref, upd_ref, h1, u, u12):
    dp, z, h, x = spot()
    c, y = dp % 2, dp // 2
    first_col = (z * 8 + h * 4 + x) * 512
    damp = aux_ref[1:2, :]

    def damped(value, first_row):
        row = first_row + lax.broadcasted_iota(jnp.int32, value.shape, 0)
        col = first_col + lax.broadcasted_iota(jnp.int32, value.shape, 1)
        return value + jnp.where(row == col, damp, 0.0)

    mine = pl.multiple_of(512 * c, 512)
    theirs = pl.multiple_of(512 * (1 - c), 512)
    h1[pl.ds(mine, 512), :] = damped(f_ref[0:512, :], mine)
    h1[pl.ds(theirs, 512), :] = damped(e_ref[0:512, :], theirs)

    @pl.when(y == 0)
    def _():
        hess_ref[...] = h1[pl.ds(mine, 512), :]

    @pl.when(y == 1)
    def _():
        a = pl.multiple_of(256 * c, 256)
        b = pl.multiple_of(256 * (1 - c), 256)
        hess_ref[pl.ds(a, 256), :] = damped(f_ref[pl.ds(512 + a, 256), :], 1024 + 512 * c + a)
        hess_ref[pl.ds(b, 256), :] = damped(e_ref[512:768, :], 1024 + 512 * c + b)

    cols12 = pl.ds(pl.multiple_of(1024 + 256 * c, 256), 256)
    for k in range(8):
        rows = slice(128 * k, 128 * k + 128)
        left = inv_ref[rows, 0:128 * k + 128]
        u[rows, :] = dot(left, h1[0:128 * k + 128, :])
        u12[rows, :] = dot(left, g_ref[0:128 * k + 128, cols12])
    fac_ref[...] = u[pl.ds(pl.multiple_of(256 * dp, 256), 256), :]
    second = damped(f_ref[pl.ds(pl.multiple_of(512 + 256 * y, 256), 256), :], 1024 + 256 * dp)
    upd_ref[...] = second - dot_t(u12[...], u[...], HI)


def finish(inv, g, final, extra, aux):
    return pl.pallas_call(
        finish_kernel,
        out_shape=(
            jax.ShapeDtypeStruct((512, 512), F32),
            jax.ShapeDtypeStruct((256, 512), F32),
            jax.ShapeDtypeStruct((256, 512), F32),
        ),
        in_specs=[VM] * 5,
        out_specs=(VM, VM, VM),
        scratch_shapes=[
            pltpu.VMEM((1024, 512), F32),
            pltpu.VMEM((1024, 512), F32),
            pltpu.VMEM((1024, 256), F32),
        ],
        compiler_params=params(),
        name="finish_rows",
    )(inv, g, final, extra, aux)


def body(hidden_states, norm_gain, damping):
    aux = jnp.concatenate(
        [norm_gain.astype(F32)[None], damping[None], jnp.zeros((6, norm_gain.shape[0]), F32)], axis=0
    )
    w, auxs, ssq = spread(hidden_states, aux)
    slab, share = gram(w, auxs, ssq, hidden_states, aux)
    g, chip = join(slab, share)
    g = g.reshape(PANEL, 1536)
    far = lax.ppermute(chip, "dp", [(0, 2), (2, 0), (1, 3), (3, 1)])
    inv = factor(g, auxs)
    final = chip + far
    core = lax.axis_index("dp") % 2
    block = lax.dynamic_slice_in_dim(final, 512 + 256 * (1 - core), 256, 0)
    extra = lax.ppermute(
        jnp.concatenate([final[:512], block], axis=0), "dp", [(0, 1), (1, 0), (2, 3), (3, 2)]
    )
    return finish(inv, g, final, extra, aux)


def solution(mesh):
    return jax.shard_map(
        body,
        mesh=mesh,
        in_specs=(P("dp", "mp"), P("mp"), P("mp")),
        out_specs=(P("dp", "mp"), P("dp", "mp"), P("dp", "mp")),
        check_vma=False,
    )
```

```python
import functools

import jax
import jax.numpy as jnp
from jax import lax
from jax.experimental import pallas as pl
from jax.experimental.pallas import tpu as pltpu
from jax.sharding import PartitionSpec as P

D = 16384
PANEL = 1024
TOKENS = 4096
MESH = pl.DeviceIdType.MESH
HI = lax.Precision.HIGHEST
F32 = jnp.float32
BF16 = jnp.bfloat16
VM = pl.BlockSpec(memory_space=pltpu.VMEM)


def params(**kw):
    return pltpu.CompilerParams(vmem_limit_bytes=60 * 2**20, **kw)


def spot():
    mp = lax.axis_index("mp")
    return lax.axis_index("dp"), mp // 8, (mp // 4) % 2, mp % 4


def at(dp, z, h, x):
    return (dp, z * 8 + h * 4 + x)


def greet(partners):
    barrier = pltpu.get_barrier_semaphore()
    for p in partners:
        pl.semaphore_signal(barrier, inc=1, device_id=p, device_id_type=MESH)
    pl.semaphore_wait(barrier, len(partners))


def dot_t(a, b, precision=None):
    return lax.dot_general(a, b, (((0,), (0,)), ((), ())), precision=precision, preferred_element_type=F32)


def dot(a, b):
    return jnp.dot(a, b, precision=HI, preferred_element_type=F32)


def parts(v):
    a = v.astype(BF16)
    r = v - a.astype(F32)
    b = r.astype(BF16)
    return a, b, (r - b.astype(F32)).astype(BF16)


def left_of(p, axis):
    a, b, c = p
    return jnp.concatenate([a, a, a, b, b, c], axis=axis)


def right_of(p, axis):
    a, b, c = p
    return jnp.concatenate([a, b, c, a, b, a], axis=axis)


def dot6(a, b):
    return jnp.dot(left_of(parts(a), 1), right_of(parts(b), 0), preferred_element_type=F32)


def lane_of(v, j):
    return jnp.broadcast_to(v[:, j:j + 1], (8, 128))


def row_of(v, r):
    return jnp.broadcast_to(v[r:r + 1, :], (8, 128))


def factor_block(groups, lane, sub, hook):
    done = [None] * 16
    groups = list(groups)
    for p in range(16):
        base = 8 * p
        here = groups[p]
        inside = (lane >= base) & (lane < base + 8)
        cols = [lane_of(here, base + t) for t in range(8)]
        a = {(r, t): row_of(cols[t], r) for t in range(8) for r in range(t + 1)}
        opened = jnp.where(inside, jnp.where(lane - base == sub, 1.0, 0.0), here)
        rows = [row_of(opened, r) for r in range(8)]
        has_next = p + 1 < 16
        if has_next:
            next_cols = [lane_of(groups[p + 1], base + t) for t in range(8)]
            next_group = jnp.where(inside, 0.0, groups[p + 1])
        m, inv = {}, {}
        out = jnp.zeros((8, 128), F32)
        for s in range(8):
            inv[s] = 1.0 / a[s, s]
            out = jnp.where(sub == s, rows[s] * lax.rsqrt(a[s, s]), out)
            for t in range(s + 1, 8):
                m[s, t] = a[s, t] * inv[s]
                for u in range(t, 8):
                    a[t, u] = a[t, u] - m[s, t] * a[s, u]
            if has_next:
                next_group = next_group - (next_cols[s] * inv[s]) * rows[s]
            for t in range(s + 1, 8):
                rows[t] = rows[t] - m[s, t] * rows[s]
                if has_next:
                    next_cols[t] = next_cols[t] - m[s, t] * next_cols[s]
        done[p] = out
        if p + 2 < 16:
            back = [None] * 8
            for s in range(7, -1, -1):
                g = rows[s] * inv[s]
                for t in range(s + 1, 8):
                    g = g - m[s, t] * back[t]
                back[s] = g
            for i in range(p + 2, 16):
                v = jnp.where(inside, 0.0, groups[i])
                for t in range(8):
                    v = v - lane_of(groups[i], base + t) * back[t]
                groups[i] = v
        if has_next:
            groups[p + 1] = next_group
        hook(p)
    return jnp.concatenate(done, axis=0)


def factor_panel(a_ref, d_ref, xl_ref, xr_ref, li_ref, inv_ref, after):
    n, blocks = PANEL, PANEL // 128
    lane = lax.broadcasted_iota(jnp.int32, (8, 128), 1)
    sub = lax.broadcasted_iota(jnp.int32, (8, 128), 0)
    row = lax.broadcasted_iota(jnp.int32, (128, 128), 0)
    col = lax.broadcasted_iota(jnp.int32, (128, 128), 1)
    wide = lax.broadcasted_iota(jnp.int32, (128, n), 1)
    wide_row = lax.broadcasted_iota(jnp.int32, (128, n), 0)

    def rows_of(k):
        kb = pl.multiple_of(128 * k, 128)
        own = (wide >= kb) & (wide < kb + 128)
        r = jnp.where(own, jnp.where(wide - kb == wide_row, 1.0, 0.0), a_ref[pl.ds(kb, 128), :])
        v = dot6(li_ref[...], r)
        inv_ref[pl.ds(kb, 128), :] = jnp.where(wide < kb + 128, v, 0.0)
        return v

    d_ref[...] = a_ref[0:128, 0:128]
    li_ref[...] = jnp.zeros((128, 128), F32)

    def turn(k, carry):
        kb = pl.multiple_of(128 * k, 128)
        groups = [d_ref[8 * i:8 * i + 8, :] for i in range(16)]
        prev = jnp.maximum(k - 1, 0)
        pb = pl.multiple_of(128 * prev, 128)
        v = parts(rows_of(prev))
        xl_ref[...] = left_of(v, 0)
        xr_ref[...] = right_of(v, 0)
        gone = (wide >= pb) & (wide < pb + 128)

        def hook(p):
            if not 1 <= p <= 14:
                return
            i, half = 1 + (p - 1) // 2, (p - 1) % 2
            rows, cols = slice(128 * i, 128 * i + 128), slice(512 * half, 512 * half + 512)
            on = (i >= k) & (k > 0)
            old = a_ref[rows, cols]
            new = jnp.where(gone[:, cols], 0.0, old) - dot_t(xl_ref[:, rows], xr_ref[:, cols])
            a_ref[rows, cols] = jnp.where(on, new, old)

        li = jnp.where(row >= col, factor_block(groups, lane, sub, hook), 0.0)
        li_ref[...] = li
        nb = pl.multiple_of(128 * jnp.minimum(k + 1, blocks - 1), 128)
        v = parts(dot6(li, a_ref[pl.ds(kb, 128), pl.ds(nb, 128)]))
        d_ref[...] = a_ref[pl.ds(nb, 128), pl.ds(nb, 128)] - dot_t(left_of(v, 0), right_of(v, 0))
        after(k)
        return carry

    lax.fori_loop(0, blocks, turn, 0)
    rows_of(blocks - 1)


def main_kernel(x_ref, aux_ref, inv_ref, h12_ref, f_ref, e_ref,
                w, auxs, sx, sz, sh, wn, xn, rms, wide, share, share_in, share_sum, share_y, g,
                slab, other, chip, far, a, d, xl, xr, li, ss, rs):
    dp, z, h, x = spot()
    c, y = dp % 2, dp // 2
    column = [at(dp, (z + q // 2) % 4, (h + q % 2) % 2, x) for q in range(1, 8)]
    ring_x = [at(dp, z, h, (x + j) % 4) for j in range(1, 4)]
    ring_z = [at(dp, (z + j) % 4, h, x) for j in range(1, 4)]
    peer_h = at(dp, z, 1 - h, x)
    peer_c = at(y * 2 + 1 - c, z, h, x)
    peer_y = at((1 - y) * 2 + c, z, h, x)
    greet(column + ring_x + [peer_c, peer_y])
    sent = []

    def copy(src, dst, i, dev, to=None):
        k = pltpu.make_async_remote_copy(src_ref=src, dst_ref=dst, send_sem=ss.at[i],
                                         recv_sem=rs.at[i if to is None else to],
                                         device_id=dev, device_id_type=MESH)
        return k

    def start(copies):
        for k in copies:
            k.start()
            sent.append(k)

    def arrive(copies):
        for k in copies:
            k.wait_recv()

    is_source = (z == 0) & (h == 0)

    def scatter(q):
        b = (q // 2) * 128 + (q % 2) * 64
        dev = column[q - 1]
        return [
            copy(aux_ref, auxs.at[x], 3 * q, dev, 0),
            copy(x_ref.at[pl.ds(512 + b, 64)], w.at[x, pl.ds(512 + b, 64)], 3 * q + 1, dev, 1),
            copy(x_ref.at[pl.ds(b, 64)], w.at[x, pl.ds(b, 64)], 3 * q + 2, dev, 2),
        ]

    @pl.when(is_source)
    def _():
        for q in range(1, 8):
            for k in scatter(q):
                k.start()
        w[x, 0:64] = x_ref[0:64]
        w[x, 512:576] = x_ref[512:576]
        auxs[x] = aux_ref[...]

    part = jnp.zeros((1024, 128), F32)
    for i in range(4):
        v = x_ref[:, 128 * i:128 * i + 128].astype(F32)
        part = part + v * v
    line = jnp.sum(part.T, axis=0, keepdims=True)
    for i in range(8):
        sx[x, i:i + 1, :] = line[:, 128 * i:128 * i + 128]
    sum_x = [copy(sx.at[x], sx.at[x], 47 + j, ring_x[j]) for j in range(3)]
    start(sum_x)

    @pl.when(jnp.logical_not(is_source))
    def _():
        arrive(scatter(1))

    own = pl.multiple_of(z * 128 + h * 64, 64)
    own_a, own_b = w.at[x, pl.ds(own, 64)], w.at[x, pl.ds(512 + own, 64)]
    step_2b = [copy(own_b, own_b, 26 + q, column[q - 1]) for q in range(1, 8)]
    step_2a = [copy(own_a, own_a, 24 + j, ring_x[j]) for j in range(3)]
    step_aux = [copy(auxs.at[x], auxs.at[x], 34 + j, ring_x[j]) for j in range(3)]
    start(step_2a + step_2b + step_aux)
    arrive(sum_x)
    sz[z] = (sx[0] + sx[1]) + (sx[2] + sx[3])
    sum_z = [copy(sz.at[z], sz.at[z], 50 + j, ring_z[j]) for j in range(3)]
    start(sum_z)
    all_a, all_b = w.at[:, pl.ds(own, 64)], w.at[x, pl.ds(512, 512)]
    step_3a = [copy(all_a, all_a, 36 + q, column[q - 1]) for q in range(1, 8)]
    step_3b = [copy(all_b, all_b, 44 + j, ring_x[j]) for j in range(3)]
    arrive(step_2a)
    start(step_3a)
    arrive(step_2b)
    start(step_3b)
    arrive(sum_z)
    sh[h] = (sz[0] + sz[1]) + (sz[2] + sz[3])
    sum_h = [copy(sh.at[h], sh.at[h], 53, peer_h)]
    start(sum_h)
    arrive(sum_h)

    inverse = lax.rsqrt((sh[0] + sh[1]) / D + 1e-05)
    for i in range(8):
        rms[128 * i:128 * i + 128, :] = jnp.broadcast_to(inverse[i:i + 1, :], (128, 128)).T

    @pl.loop(0, 8)
    def _(i):
        rows = pl.ds(pl.multiple_of(i * 128, 128), 128)
        scale = jnp.concatenate([rms[rows, :]] * 4, axis=1)
        xn[rows, :] = (x_ref[rows, :].astype(F32) * scale * aux_ref[0:1, :]).astype(BF16)

    arrive(step_aux)
    arrive(step_3a)
    arrive(step_3b)

    @pl.loop(0, 8)
    def _(i):
        rows = pl.ds(pl.multiple_of(i * 128, 128), 128)
        scale = jnp.concatenate([rms[rows, :]] * 4, axis=1)
        for b in range(4):
            wn[b, rows, :] = (w[b, rows, :].astype(F32) * scale * auxs[b, 0:1, :]).astype(BF16)

    s = z * 4 + x
    strip = wn[s // 8, :, pl.ds(pl.multiple_of(((s % 8) // 2) * 128, 128), 128)]
    for b in range(4):
        wide[:, 512 * b:512 * b + 512] = dot_t(strip, wn[b]) * (1.0 / TOKENS)
    share[...] = wide[pl.ds(pl.multiple_of((s % 2) * 64, 64), 64), :]
    to_core = [copy(share.at[pl.ds(pl.multiple_of(32 * (1 - c), 32), 32)], share_in, 54, peer_c)]
    start(to_core)

    def slab_rows(lo, hi):
        @pl.loop(lo, hi)
        def _(i):
            left = wn[i // 4, :, pl.ds(pl.multiple_of((i % 4) * 128, 128), 128)]
            slab[pl.ds(pl.multiple_of(i * 128, 128), 128), :] = dot_t(left, xn[...]) * (1.0 / TOKENS)

    slab_rows(0, 4)
    arrive(to_core)
    share_sum[...] = share[pl.ds(pl.multiple_of(32 * c, 32), 32), :] + share_in[...]
    give = pl.ds(pl.multiple_of(1024 + 512 * (1 - y), 512), 512)
    keep = pl.ds(pl.multiple_of(1024 + 512 * y, 512), 512)
    to_y = [copy(share_sum.at[:, pl.ds(0, 1024)], share_y.at[:, pl.ds(0, 1024)], 55, peer_y)]
    to_y2 = [copy(share_sum.at[:, give], share_y.at[:, pl.ds(1024, 512)], 56, peer_y)]
    start(to_y + to_y2)
    slab_rows(4, 16)
    arrive(to_y)
    g[z, x, c] = share_sum[:, 0:1024] + share_y[:, 0:1024]
    first, second = pl.ds(0, 16), pl.ds(16, 16)

    def gather_1(ref, i):
        one_a, one_b = ref.at[z, x, c, first], ref.at[z, x, c, second]
        return ([copy(one_a, one_a, i + j, ring_x[j]) for j in range(3)],
                [copy(one_b, one_b, i + 3 + j, ring_z[j]) for j in range(3)])

    def gather_2(ref, i):
        row_a, row_b = ref.at[z, :, c, first], ref.at[:, x, c, second]
        return ([copy(row_a, row_a, i + j, ring_z[j]) for j in range(3)],
                [copy(row_b, row_b, i + 3 + j, ring_x[j]) for j in range(3)])

    g1, g2 = gather_1(g, 57), gather_2(g, 63)
    g_core = [copy(g.at[:, :, c, k], g.at[:, :, c, k], i, peer_c) for k, i in ((first, 69), (second, 70))]
    q1, q2 = gather_1(h12_ref, 75), gather_2(h12_ref, 81)
    q_core = [copy(h12_ref.at[:, :, c], h12_ref.at[:, :, c], 87, peer_c)]
    start(g1[0] + g1[1])
    spans = [(512 * (1 - c), 0, 512), (1024 + 256 * (1 - c), 512, 256), (1536 + 256 * (1 - c), 768, 256)]
    slabs = [
        copy(slab.at[pl.ds(pl.multiple_of(p, 256), n)], other.at[pl.ds(b, n)], 71 + i, peer_c)
        for i, (p, b, n) in enumerate(spans)
    ]
    start(slabs)
    arrive(g1[0])
    start(g2[0])
    arrive(g1[1])
    start(g2[1])
    arrive(to_y2)
    h12_ref[z, x, c] = share_sum[:, keep] + share_y[:, 1024:1536]
    arrive(slabs)
    chip[0:512, :] = slab[pl.ds(pl.multiple_of(512 * c, 512), 512), :] + other[0:512, :]
    chip[512:768, :] = slab[pl.ds(pl.multiple_of(1024 + 256 * c, 256), 256), :] + other[512:768, :]
    chip[768:1024, :] = slab[pl.ds(pl.multiple_of(1536 + 256 * c, 256), 256), :] + other[768:1024, :]
    slab_y = [copy(chip, far, 74, peer_y)]
    arrive(g2[0])
    start(g_core[:1])
    arrive(g2[1])
    start(g_core[1:])
    start(slab_y + q1[0] + q1[1])
    arrive(g_core)
    for i in range(4):
        for j in range(4):
            for k in range(2):
                lo = 64 * (4 * i + j) + 32 * k
                a[lo:lo + 32, :] = g[i, j, k]
    row = lax.broadcasted_iota(jnp.int32, (128, 128), 0)
    col = lax.broadcasted_iota(jnp.int32, (128, 128), 1)
    for k in range(8):
        at_k = slice(128 * k, 128 * k + 128)
        damp = auxs[k // 4, 1:2, 128 * (k % 4):128 * (k % 4) + 128]
        a[at_k, at_k] = a[at_k, at_k] + jnp.where(row == col, damp, 0.0)

    block = pl.multiple_of(512 + 256 * (1 - c), 256)
    to_e = [copy(f_ref.at[pl.ds(0, 512)], e_ref.at[pl.ds(0, 512)], 88, peer_c),
            copy(f_ref.at[pl.ds(block, 256)], e_ref.at[pl.ds(512, 256)], 89, peer_c)]

    def after(k):
        @pl.when(k == 1)
        def _():
            arrive(q1[0])
            arrive(q1[1])
            for m in q2[0] + q2[1]:
                m.start()

        @pl.when(k == 4)
        def _():
            arrive(q2[0])
            arrive(q2[1])
            for m in q_core:
                m.start()

        @pl.when(k == 6)
        def _():
            arrive(slab_y)
            f_ref[...] = chip[...] + far[...]
            for m in to_e:
                m.start()

    factor_panel(a, d, xl, xr, li, inv_ref, after)
    arrive(q_core + to_e)
    for k in sent + q2[0] + q2[1] + q_core + to_e:
        k.wait_send()

    @pl.when(is_source)
    def _():
        for q in range(1, 8):
            for k in scatter(q):
                k.wait_send()


def main(hidden, aux):
    def f32(*shape):
        return pltpu.VMEM(shape, F32)

    def b16(*shape):
        return pltpu.VMEM(shape, BF16)

    return pl.pallas_call(
        main_kernel,
        out_shape=(
            jax.ShapeDtypeStruct((PANEL, PANEL), F32),
            jax.ShapeDtypeStruct((4, 4, 2, 32, 512), F32),
            jax.ShapeDtypeStruct((1024, 512), F32),
            jax.ShapeDtypeStruct((768, 512), F32),
        ),
        in_specs=[VM, VM],
        out_specs=(VM, VM, VM, VM),
        scratch_shapes=[
            b16(4, 1024, 512), f32(4, 8, 512), f32(4, 8, 128), f32(4, 8, 128), f32(2, 8, 128),
            b16(4, 1024, 512), b16(1024, 512), f32(1024, 128), f32(128, 2048), f32(64, 2048),
            f32(32, 2048), f32(32, 2048), f32(32, 1536), f32(4, 4, 2, 32, 1024),
            f32(2048, 512), f32(1024, 512), f32(1024, 512), f32(1024, 512),
            f32(PANEL, PANEL), f32(128, 128), b16(768, PANEL), b16(768, PANEL), f32(128, 128),
            pltpu.SemaphoreType.DMA((90,)),
            pltpu.SemaphoreType.DMA((90,)),
        ],
        compiler_params=params(collective_id=0, has_side_effects=True),
        name="window_panel",
    )(hidden, aux)


def finish_kernel(inv_ref, g_ref, f_ref, e_ref, aux_ref, hess_ref, fac_ref, upd_ref, h1, u, u12):
    dp, z, h, x = spot()
    c, y = dp % 2, dp // 2
    first_col = (z * 8 + h * 4 + x) * 512
    damp = aux_ref[1:2, :]

    def damped(value, first_row):
        row = first_row + lax.broadcasted_iota(jnp.int32, value.shape, 0)
        col = first_col + lax.broadcasted_iota(jnp.int32, value.shape, 1)
        return value + jnp.where(row == col, damp, 0.0)

    mine = pl.multiple_of(512 * c, 512)
    theirs = pl.multiple_of(512 * (1 - c), 512)
    h1[pl.ds(mine, 512), :] = damped(f_ref[0:512, :], mine)
    h1[pl.ds(theirs, 512), :] = damped(e_ref[0:512, :], theirs)

    @pl.when(y == 0)
    def _():
        hess_ref[...] = h1[pl.ds(mine, 512), :]

    @pl.when(y == 1)
    def _():
        a = pl.multiple_of(256 * c, 256)
        b = pl.multiple_of(256 * (1 - c), 256)
        hess_ref[pl.ds(a, 256), :] = damped(f_ref[pl.ds(512 + a, 256), :], 1024 + 512 * c + a)
        hess_ref[pl.ds(b, 256), :] = damped(e_ref[512:768, :], 1024 + 512 * c + b)

    cols12 = pl.ds(pl.multiple_of(256 * c, 256), 256)
    for k in range(8):
        rows = slice(128 * k, 128 * k + 128)
        left = inv_ref[rows, 0:128 * k + 128]
        u[rows, :] = dot(left, h1[0:128 * k + 128, :])
        u12[rows, :] = dot(left, g_ref[0:128 * k + 128, cols12])
    fac_ref[...] = u[pl.ds(pl.multiple_of(256 * dp, 256), 256), :]
    second = damped(f_ref[pl.ds(pl.multiple_of(512 + 256 * y, 256), 256), :], 1024 + 256 * dp)
    upd_ref[...] = second - dot_t(u12[...], u[...], HI)


def finish(inv, g, final, extra, aux):
    return pl.pallas_call(
        finish_kernel,
        out_shape=(
            jax.ShapeDtypeStruct((512, 512), F32),
            jax.ShapeDtypeStruct((256, 512), F32),
            jax.ShapeDtypeStruct((256, 512), F32),
        ),
        in_specs=[VM] * 5,
        out_specs=(VM, VM, VM),
        scratch_shapes=[
            pltpu.VMEM((1024, 512), F32),
            pltpu.VMEM((1024, 512), F32),
            pltpu.VMEM((1024, 256), F32),
        ],
        compiler_params=params(),
        name="finish_rows",
    )(inv, g, final, extra, aux)


def body(hidden_states, norm_gain, damping):
    aux = jnp.concatenate(
        [norm_gain.astype(F32)[None], damping[None], jnp.zeros((6, norm_gain.shape[0]), F32)], axis=0
    )
    inv, h12, final, extra = main(hidden_states, aux)
    return finish(inv, h12.reshape(PANEL, 512), final, extra, aux)


def solution(mesh):
    return jax.shard_map(
        body,
        mesh=mesh,
        in_specs=(P("dp", "mp"), P("mp"), P("mp")),
        out_specs=(P("dp", "mp"), P("dp", "mp"), P("dp", "mp")),
        check_vma=False,
    )
```

```python
import jax
import jax.numpy as jnp
from jax import lax
from jax.experimental import pallas as pl
from jax.experimental.pallas import tpu as pltpu
from jax.sharding import PartitionSpec as P

D = 16384
PANEL = 1024
TOKENS = 4096
MESH = pl.DeviceIdType.MESH
F32 = jnp.float32
BF16 = jnp.bfloat16
VM = pl.BlockSpec(memory_space=pltpu.VMEM)


def params(**kw):
    return pltpu.CompilerParams(vmem_limit_bytes=60 * 2**20, **kw)


def spot():
    mp = lax.axis_index("mp")
    return lax.axis_index("dp"), mp // 8, (mp // 4) % 2, mp % 4


def at(dp, z, h, x):
    return (dp, z * 8 + h * 4 + x)


def greet_signal(partners):
    barrier = pltpu.get_barrier_semaphore()
    for p in partners:
        pl.semaphore_signal(barrier, inc=1, device_id=p, device_id_type=MESH)


def greet_wait(count):
    pl.semaphore_wait(pltpu.get_barrier_semaphore(), count)


def dot_t(a, b):
    return lax.dot_general(a, b, (((0,), (0,)), ((), ())), preferred_element_type=F32)


def parts(v):
    a = v.astype(BF16)
    r = v - a.astype(F32)
    b = r.astype(BF16)
    return a, b, (r - b.astype(F32)).astype(BF16)


def whole_parts(v):
    v = jnp.concatenate([v, jnp.zeros_like(v)], axis=0)
    return parts(v)


def left_of(p, axis):
    a, b, c = p
    return jnp.concatenate([a, a, a, b, b, c], axis=axis)


def right_of(p, axis):
    a, b, c = p
    return jnp.concatenate([a, b, c, a, b, a], axis=axis)


def two_parts(v):
    a = v.astype(BF16)
    return a, (v - a.astype(F32)).astype(BF16)


def dot6(a, b):
    return jnp.dot(left_of(parts(a), 1), right_of(parts(b), 0), preferred_element_type=F32)


def lane_of(v, j):
    return jnp.broadcast_to(v[:, j:j + 1], (8, 128))


def row_of(v, r):
    return jnp.broadcast_to(v[r:r + 1, :], (8, 128))


def factor_block(groups, lane, sub, hook):
    done = [None] * 16
    groups = list(groups)
    for p in range(16):
        base = 8 * p
        here = groups[p]
        inside = (lane >= base) & (lane < base + 8)
        cols = [lane_of(here, base + t) for t in range(8)]
        a = {(r, t): row_of(cols[t], r) for t in range(8) for r in range(t + 1)}
        opened = jnp.where(inside, jnp.where(lane - base == sub, 1.0, 0.0), here)
        rows = [row_of(opened, r) for r in range(8)]
        has_next = p + 1 < 16
        if has_next:
            next_cols = [lane_of(groups[p + 1], base + t) for t in range(8)]
            next_group = jnp.where(inside, 0.0, groups[p + 1])
        m, inv = {}, {}
        out = jnp.zeros((8, 128), F32)
        for s in range(8):
            inv[s] = 1.0 / a[s, s]
            out = jnp.where(sub == s, rows[s] * lax.rsqrt(a[s, s]), out)
            for t in range(s + 1, 8):
                m[s, t] = a[s, t] * inv[s]
                for u in range(t, 8):
                    a[t, u] = a[t, u] - m[s, t] * a[s, u]
            if has_next:
                next_group = next_group - (next_cols[s] * inv[s]) * rows[s]
            for t in range(s + 1, 8):
                rows[t] = rows[t] - m[s, t] * rows[s]
                if has_next:
                    next_cols[t] = next_cols[t] - m[s, t] * next_cols[s]
        done[p] = out
        if p + 2 < 16:
            v = whole_parts(out)
            product = dot_t(left_of(v, 0), right_of(v, 0))
            for i in range(p + 2, 16):
                groups[i] = jnp.where(inside, 0.0, groups[i]) - product[8 * i:8 * i + 8, :]
        if has_next:
            groups[p + 1] = next_group
        hook(p)
    return jnp.concatenate(done, axis=0)


def factor_panel(a_ref, d_ref, xl_ref, xr_ref, li_ref, inv_ref, after):
    n, blocks = PANEL, PANEL // 128
    lane = lax.broadcasted_iota(jnp.int32, (8, 128), 1)
    sub = lax.broadcasted_iota(jnp.int32, (8, 128), 0)
    row = lax.broadcasted_iota(jnp.int32, (128, 128), 0)
    col = lax.broadcasted_iota(jnp.int32, (128, 128), 1)
    wide = lax.broadcasted_iota(jnp.int32, (128, n), 1)
    wide_row = lax.broadcasted_iota(jnp.int32, (128, n), 0)

    def rows_of(k):
        kb = pl.multiple_of(128 * k, 128)
        own = (wide >= kb) & (wide < kb + 128)
        r = jnp.where(own, jnp.where(wide - kb == wide_row, 1.0, 0.0), a_ref[pl.ds(kb, 128), :])
        v = dot6(li_ref[...], r)
        inv_ref[pl.ds(kb, 128), :] = jnp.where(wide < kb + 128, v, 0.0)
        return v

    d_ref[...] = a_ref[0:128, 0:128]
    li_ref[...] = jnp.zeros((128, 128), F32)

    def turn(k, carry):
        kb = pl.multiple_of(128 * k, 128)
        groups = [d_ref[8 * i:8 * i + 8, :] for i in range(16)]
        prev = jnp.maximum(k - 1, 0)
        pb = pl.multiple_of(128 * prev, 128)
        v = rows_of(prev)
        xl_ref[...] = left_of(parts(v.T), 1)
        xr_ref[...] = right_of(parts(v), 0)

        def hook(p):
            if not 1 <= p <= 8:
                return
            top, first = 128 + 448 * ((p - 1) % 2), 256 * ((p - 1) // 2)
            rows, cols = slice(top, top + 448), slice(first, first + 256)
            below = (top + lax.broadcasted_iota(jnp.int32, (448, 256), 0) >= kb) & (k > 0)
            at_col = first + lax.broadcasted_iota(jnp.int32, (448, 256), 1)
            gone = (at_col >= pb) & (at_col < pb + 128)
            old = a_ref[rows, cols]
            new = jnp.where(gone, 0.0, old) - jnp.dot(
                xl_ref[rows, :], xr_ref[:, cols], preferred_element_type=F32
            )
            a_ref[rows, cols] = jnp.where(below, new, old)

        li = jnp.where(row >= col, factor_block(groups, lane, sub, hook), 0.0)
        li_ref[...] = li
        nb = pl.multiple_of(128 * jnp.minimum(k + 1, blocks - 1), 128)
        v = parts(dot6(li, a_ref[pl.ds(kb, 128), pl.ds(nb, 128)]))
        d_ref[...] = a_ref[pl.ds(nb, 128), pl.ds(nb, 128)] - dot_t(left_of(v, 0), right_of(v, 0))
        after(k)
        return carry

    lax.fori_loop(0, blocks, turn, 0)
    rows_of(blocks - 1)


def main_kernel(x_ref, aux_ref, hess_ref, fac_ref, upd_ref,
                xs, w, auxs, sx, sz, wn, xn, rms, wide, share, share_in, share_sum, share_y, g,
                slab, other, chip, far, a, d, xl, xr, li, inv, h12, final, extra, h1, hp, hq, u, ss, rs):
    dp, z, h, x = spot()
    c, y = dp % 2, dp // 2
    column = [at(dp, (z + q // 2) % 4, (h + q % 2) % 2, x) for q in range(1, 8)]
    ring_x = [at(dp, z, h, (x + j) % 4) for j in range(1, 4)]
    ring_z = [at(dp, (z + j) % 4, h, x) for j in range(1, 4)]
    peer_c = at(y * 2 + 1 - c, z, h, x)
    peer_y = at((1 - y) * 2 + c, z, h, x)
    greet_signal(column + ring_x + [peer_c, peer_y])
    sent = []

    def copy(src, dst, i, dev, to=None):
        k = pltpu.make_async_remote_copy(src_ref=src, dst_ref=dst, send_sem=ss.at[i],
                                         recv_sem=rs.at[i if to is None else to],
                                         device_id=dev, device_id_type=MESH)
        return k

    def start(copies):
        for k in copies:
            k.start()
            sent.append(k)

    def arrive(copies):
        for k in copies:
            k.wait_recv()

    part = jnp.zeros((1024, 128), F32)
    for i in range(4):
        v = x_ref[:, 128 * i:128 * i + 128].astype(F32)
        part = part + v * v
    line = jnp.sum(part.T, axis=0, keepdims=True)
    for i in range(8):
        sx[x, i:i + 1, :] = line[:, 128 * i:128 * i + 128]
    is_source = (z == 0) & (h == 0)

    @pl.when(is_source)
    def _():
        own_damp = [v.astype(F32) for v in parts(aux_ref[1:2, :])]
        extra_rows = jnp.concatenate([aux_ref[0:1, :]] + own_damp + [jnp.zeros((12, 512), F32)], axis=0)
        for q in range(8):
            xs[q, 0:16, :] = extra_rows.astype(BF16)
            xs[q, 16:144, :] = x_ref[128 * q:128 * q + 128, :]
        w[x, 0] = xs[0]

    greet_wait(12)
    sum_x = [copy(sx.at[x], sx.at[x], 47 + j, ring_x[j]) for j in range(3)]
    start(sum_x)

    def scatter(q):
        return copy(xs.at[q], w.at[x, q], q, column[q - 1], 0)

    @pl.when(is_source)
    def _():
        for q in range(1, 8):
            scatter(q).start()

    own = z * 2 + h

    @pl.when(jnp.logical_not(is_source))
    def _():
        copy(xs.at[0], w.at[x, own], 0, column[0], 0).wait_recv()

    own_a, own_b = w.at[x, own, pl.ds(0, 80)], w.at[x, own, pl.ds(80, 64)]
    step_2b = [copy(own_b, own_b, 26 + q, column[q - 1]) for q in range(1, 8)]
    step_2a = [copy(own_a, own_a, 24 + j, ring_x[j]) for j in range(3)]
    start(step_2a + step_2b)
    arrive(sum_x)
    sz[own] = (sx[0] + sx[1]) + (sx[2] + sx[3])
    sum_c = [copy(sz.at[own], sz.at[own], 91 + q, column[q - 1]) for q in range(1, 8)]
    start(sum_c)
    all_a, all_b = w.at[:, own, pl.ds(16, 64)], w.at[x, :, pl.ds(80, 64)]
    step_3a = [copy(all_a, all_a, 36 + q, column[q - 1]) for q in range(1, 8)]
    step_3b = [copy(all_b, all_b, 44 + j, ring_x[j]) for j in range(3)]
    arrive(step_2a)
    start(step_3a)
    arrive(step_2b)
    start(step_3b)
    arrive(sum_c)

    total = ((sz[0] + sz[1]) + (sz[2] + sz[3])) + ((sz[4] + sz[5]) + (sz[6] + sz[7]))
    inverse = lax.rsqrt(total / D + 1e-05)
    for i in range(8):
        rms[128 * i:128 * i + 128, :] = jnp.broadcast_to(inverse[i:i + 1, :], (128, 128)).T

    @pl.loop(0, 8)
    def _(i):
        rows = pl.ds(pl.multiple_of(i * 128, 128), 128)
        scale = jnp.concatenate([rms[rows, :]] * 4, axis=1)
        xn[rows, :] = (x_ref[rows, :].astype(F32) * scale * aux_ref[0:1, :]).astype(BF16)

    for b in range(4):
        v = w[b, own, 0:16, :].astype(F32)
        auxs[b, 0:1, :] = v[0:1, :]
        auxs[b, 1:2, :] = (v[1:2, :] + v[2:3, :]) + v[3:4, :]
    arrive(step_3a)
    arrive(step_3b)

    def normalise(blocks):
        @pl.loop(0, 8)
        def _(i):
            rows = pl.ds(pl.multiple_of(i * 128, 128), 128)
            scale = jnp.concatenate([rms[rows, :]] * 4, axis=1)
            for b in blocks:
                wn[b, rows, :] = (w[b, i, 16:144, :].astype(F32) * scale * auxs[b, 0:1, :]).astype(BF16)

    s = z * 4 + x
    half = pl.ds(pl.multiple_of((s % 2) * 64, 64), 64)
    panels = [pl.ds(0, 1024), pl.ds(1024, 1024)]
    give, keep = pl.ds(pl.multiple_of(32 * (1 - c), 32), 32), pl.ds(pl.multiple_of(32 * c, 32), 32)

    def share_of(m):
        strip = wn[s // 8, :, pl.ds(pl.multiple_of(((s % 8) // 2) * 128, 128), 128)]
        for b in range(2):
            wide[:, 512 * b:512 * b + 512] = dot_t(strip, wn[2 * m + b]) * (1.0 / TOKENS)
        share[:, panels[m]] = wide[half, :]
        k = copy(share.at[give, panels[m]], share_in.at[:, panels[m]], 54 + 36 * m, peer_c)
        start([k])
        return k

    def slab_rows(b):
        slab[512 * b:512 * b + 512, :] = dot_t(wn[b], xn[...]) * (1.0 / TOKENS)

    normalise((0, 1))
    core_1 = share_of(0)
    normalise((2, 3))
    arrive([core_1])
    share_sum[:, panels[0]] = share[keep, panels[0]] + share_in[:, panels[0]]
    to_y = [copy(share_sum.at[:, panels[0]], share_y.at[:, pl.ds(0, 1024)], 55, peer_y)]
    start(to_y)
    core_2 = share_of(1)
    slab_rows(0)
    arrive(to_y)
    g[z, x, c] = share_sum[:, 0:1024] + share_y[:, 0:1024]
    first, second = pl.ds(0, 16), pl.ds(16, 16)

    def gather_1(ref, i):
        one_a, one_b = ref.at[z, x, c, first], ref.at[z, x, c, second]
        return ([copy(one_a, one_a, i + j, ring_x[j]) for j in range(3)],
                [copy(one_b, one_b, i + 3 + j, ring_z[j]) for j in range(3)])

    def gather_2(ref, i):
        row_a, row_b = ref.at[z, :, c, first], ref.at[:, x, c, second]
        return ([copy(row_a, row_a, i + j, ring_z[j]) for j in range(3)],
                [copy(row_b, row_b, i + 3 + j, ring_x[j]) for j in range(3)])

    g1, g2 = gather_1(g, 57), gather_2(g, 63)
    g_core = [copy(g.at[:, :, c, k], g.at[:, :, c, k], i, peer_c) for k, i in ((first, 69), (second, 70))]
    q1, q2 = gather_1(h12, 75), gather_2(h12, 81)
    q_core = [copy(h12.at[:, :, c], h12.at[:, :, c], 87, peer_c)]
    start(g1[0] + g1[1])
    arrive([core_2])
    share_sum[:, panels[1]] = share[keep, panels[1]] + share_in[:, panels[1]]
    far_12 = pl.ds(pl.multiple_of(1024 + 512 * (1 - y), 512), 512)
    near_12 = pl.ds(pl.multiple_of(1024 + 512 * y, 512), 512)
    to_y2 = [copy(share_sum.at[:, far_12], share_y.at[:, pl.ds(1024, 512)], 56, peer_y)]
    start(to_y2)
    slab_rows(1)
    spans = [(512 * (1 - c), 0, 512), (1024 + 256 * (1 - c), 512, 256), (1536 + 256 * (1 - c), 768, 256)]
    slabs = [
        copy(slab.at[pl.ds(pl.multiple_of(p, 256), n)], other.at[pl.ds(b, n)], 71 + i, peer_c)
        for i, (p, b, n) in enumerate(spans)
    ]
    start(slabs[:1])
    slab_y = [copy(chip.at[pl.ds(p, 512)], far.at[pl.ds(p, 512)], 73 + i, peer_y)
              for i, p in ((1, 0), (18, 512))]
    arrive(g1[0])
    start(g2[0])
    arrive(g1[1])
    start(g2[1])
    slab_rows(2)
    slab_rows(3)
    start(slabs[1:])
    arrive(to_y2)
    h12[z, x, c] = share_sum[:, near_12] + share_y[:, 1024:1536]
    arrive(slabs[:1])
    chip[0:512, :] = slab[pl.ds(pl.multiple_of(512 * c, 512), 512), :] + other[0:512, :]
    start(slab_y[:1])
    arrive(slabs[1:])
    chip[512:768, :] = slab[pl.ds(pl.multiple_of(1024 + 256 * c, 256), 256), :] + other[512:768, :]
    chip[768:1024, :] = slab[pl.ds(pl.multiple_of(1536 + 256 * c, 256), 256), :] + other[768:1024, :]
    start(slab_y[1:])
    arrive(g2[0])
    start(g_core[:1])
    arrive(g2[1])
    start(g_core[1:])
    start(q1[0] + q1[1])
    arrive(g_core)
    for i in range(4):
        for j in range(4):
            for k in range(2):
                lo = 64 * (4 * i + j) + 32 * k
                a[lo:lo + 32, :] = g[i, j, k]
    row = lax.broadcasted_iota(jnp.int32, (128, 128), 0)
    col = lax.broadcasted_iota(jnp.int32, (128, 128), 1)
    for k in range(8):
        at_k = slice(128 * k, 128 * k + 128)
        damp = auxs[k // 4, 1:2, 128 * (k % 4):128 * (k % 4) + 128]
        a[at_k, at_k] = a[at_k, at_k] + jnp.where(row == col, damp, 0.0)

    block = pl.multiple_of(512 + 256 * (1 - c), 256)
    to_e = [copy(final.at[pl.ds(0, 512)], extra.at[pl.ds(0, 512)], 88, peer_c),
            copy(final.at[pl.ds(block, 256)], extra.at[pl.ds(512, 256)], 89, peer_c)]

    def after(k):
        @pl.when(k == 1)
        def _():
            arrive(q1[0])
            arrive(q1[1])
            for m in q2[0] + q2[1]:
                m.start()

        @pl.when(k == 4)
        def _():
            arrive(q2[0])
            arrive(q2[1])
            for m in q_core:
                m.start()

        @pl.when(k == 5)
        def _():
            arrive(slab_y)
            final[...] = chip[...] + far[...]
            for m in to_e:
                m.start()

    factor_panel(a, d, xl, xr, li, inv, after)
    arrive(q_core + to_e)

    first_col = (z * 8 + h * 4 + x) * 512
    damp_own = aux_ref[1:2, :]

    def damped(value, first_row):
        rows = first_row + lax.broadcasted_iota(jnp.int32, value.shape, 0)
        cols = first_col + lax.broadcasted_iota(jnp.int32, value.shape, 1)
        return value + jnp.where(rows == cols, damp_own, 0.0)

    mine = pl.multiple_of(512 * c, 512)
    theirs = pl.multiple_of(512 * (1 - c), 512)
    h1[pl.ds(mine, 512), :] = damped(final[0:512, :], mine)
    h1[pl.ds(theirs, 512), :] = damped(extra[0:512, :], theirs)

    @pl.when(y == 0)
    def _():
        hess_ref[...] = h1[pl.ds(mine, 512), :]

    @pl.when(y == 1)
    def _():
        p = pl.multiple_of(256 * c, 256)
        q = pl.multiple_of(256 * (1 - c), 256)
        hess_ref[pl.ds(p, 256), :] = damped(final[pl.ds(512 + p, 256), :], 1024 + 512 * c + p)
        hess_ref[pl.ds(q, 256), :] = damped(extra[512:768, :], 1024 + 512 * c + q)

    for i in range(8):
        rows = slice(128 * i, 128 * i + 128)
        hp[rows, 0:512], hq[rows, 0:512] = two_parts(h1[rows, :])
        for j in range(2):
            p = 128 * i + 64 * j
            block12 = jnp.concatenate(
                [h12[i // 2, 2 * (i % 2) + j, m, :, pl.ds(pl.multiple_of(256 * c, 256), 256)] for m in range(2)], axis=0
            )
            hp[p:p + 64, 512:768], hq[p:p + 64, 512:768] = two_parts(block12)
    for i in range(2):
        rows, n = slice(512 * i, 512 * i + 512), 512 * i + 512
        p, q = two_parts(inv[rows, 0:n])
        u[rows, :] = jnp.dot(
            jnp.concatenate([p, p, q], axis=1),
            jnp.concatenate([hp[0:n, :], hq[0:n, :], hp[0:n, :]], axis=0),
            preferred_element_type=F32,
        )
    fac_ref[...] = u[pl.ds(pl.multiple_of(256 * dp, 256), 256), 0:512]
    p, q = two_parts(u[:, 512:768])
    v, r = two_parts(u[:, 0:512])
    upd_ref[...] = damped(
        final[pl.ds(pl.multiple_of(512 + 256 * y, 256), 256), :], 1024 + 256 * dp
    ) - dot_t(jnp.concatenate([p, p, q], axis=0), jnp.concatenate([v, r, v], axis=0))
    for k in sent + q2[0] + q2[1] + q_core + to_e:
        k.wait_send()

    @pl.when(is_source)
    def _():
        for q in range(1, 8):
            scatter(q).wait_send()


def main(hidden, aux):
    def f32(*shape):
        return pltpu.VMEM(shape, F32)

    def b16(*shape):
        return pltpu.VMEM(shape, BF16)

    return pl.pallas_call(
        main_kernel,
        out_shape=(
            jax.ShapeDtypeStruct((512, 512), F32),
            jax.ShapeDtypeStruct((256, 512), F32),
            jax.ShapeDtypeStruct((256, 512), F32),
        ),
        in_specs=[VM, VM],
        out_specs=(VM, VM, VM),
        scratch_shapes=[
            b16(8, 144, 512), b16(4, 8, 144, 512), f32(4, 8, 512), f32(4, 8, 128), f32(8, 8, 128),
            b16(4, 1024, 512), b16(1024, 512), f32(1024, 128), f32(128, 1024), f32(64, 2048),
            f32(32, 2048), f32(32, 2048), f32(32, 1536), f32(4, 4, 2, 32, 1024),
            f32(2048, 512), f32(1024, 512), f32(1024, 512), f32(1024, 512),
            f32(PANEL, PANEL), f32(128, 128), b16(PANEL, 768), b16(768, PANEL), f32(128, 128),
            f32(PANEL, PANEL), f32(4, 4, 2, 32, 512), f32(1024, 512), f32(768, 512),
            f32(1024, 512), b16(1024, 768), b16(1024, 768), f32(1024, 768),
            pltpu.SemaphoreType.DMA((100,)),
            pltpu.SemaphoreType.DMA((100,)),
        ],
        compiler_params=params(collective_id=0, has_side_effects=True),
        name="window_panel",
    )(hidden, aux)


def body(hidden_states, norm_gain, damping):
    aux = jnp.concatenate(
        [norm_gain.astype(F32)[None], damping[None], jnp.zeros((6, norm_gain.shape[0]), F32)], axis=0
    )
    return main(hidden_states, aux)


def solution(mesh):
    return jax.shard_map(
        body,
        mesh=mesh,
        in_specs=(P("dp", "mp"), P("mp"), P("mp")),
        out_specs=(P("dp", "mp"), P("dp", "mp"), P("dp", "mp")),
        check_vma=False,
    )
```

```python
import jax
import jax.numpy as jnp
from jax import lax
from jax.experimental import pallas as pl
from jax.experimental.pallas import tpu as pltpu
from jax.sharding import PartitionSpec as P

D = 16384
PANEL = 1024
TOKENS = 4096
MESH = pl.DeviceIdType.MESH
F32 = jnp.float32
BF16 = jnp.bfloat16
VM = pl.BlockSpec(memory_space=pltpu.VMEM)


def params(**kw):
    return pltpu.CompilerParams(vmem_limit_bytes=60 * 2**20, **kw)


def spot():
    mp = lax.axis_index("mp")
    return lax.axis_index("dp"), mp // 8, (mp // 4) % 2, mp % 4


def at(dp, z, h, x):
    return (dp, z * 8 + h * 4 + x)


def greet_signal(partners):
    barrier = pltpu.get_barrier_semaphore()
    for p in partners:
        pl.semaphore_signal(barrier, inc=1, device_id=p, device_id_type=MESH)


def greet_wait(count):
    pl.semaphore_wait(pltpu.get_barrier_semaphore(), count)


def dot_t(a, b):
    return lax.dot_general(a, b, (((0,), (0,)), ((), ())), preferred_element_type=F32)


def parts(v):
    a = v.astype(BF16)
    r = v - a.astype(F32)
    b = r.astype(BF16)
    return a, b, (r - b.astype(F32)).astype(BF16)


def whole_parts(v):
    v = jnp.concatenate([v, jnp.zeros_like(v)], axis=0)
    return parts(v)


def left_of(p, axis):
    a, b, c = p
    return jnp.concatenate([a, a, a, b, b, c], axis=axis)


def right_of(p, axis):
    a, b, c = p
    return jnp.concatenate([a, b, c, a, b, a], axis=axis)


def two_parts(v):
    a = v.astype(BF16)
    return a, (v - a.astype(F32)).astype(BF16)


def dot6(a, b):
    return jnp.dot(left_of(parts(a), 1), right_of(parts(b), 0), preferred_element_type=F32)


def lane_of(v, j):
    return jnp.broadcast_to(v[:, j:j + 1], (8, 128))


def row_of(v, r):
    return jnp.broadcast_to(v[r:r + 1, :], (8, 128))


def factor_block(groups, lane, sub, hook):
    done = [None] * 16
    groups = list(groups)
    for p in range(16):
        base = 8 * p
        here = groups[p]
        inside = (lane >= base) & (lane < base + 8)
        cols = [lane_of(here, base + t) for t in range(8)]
        a = {(r, t): row_of(cols[t], r) for t in range(8) for r in range(t + 1)}
        opened = jnp.where(inside, jnp.where(lane - base == sub, 1.0, 0.0), here)
        rows = [row_of(opened, r) for r in range(8)]
        has_next = p + 1 < 16
        if has_next:
            next_cols = [lane_of(groups[p + 1], base + t) for t in range(8)]
            next_group = jnp.where(inside, 0.0, groups[p + 1])
        m, inv = {}, {}
        out = jnp.zeros((8, 128), F32)
        for s in range(8):
            inv[s] = 1.0 / a[s, s]
            out = jnp.where(sub == s, rows[s] * lax.rsqrt(a[s, s]), out)
            for t in range(s + 1, 8):
                m[s, t] = a[s, t] * inv[s]
                for u in range(t, 8):
                    a[t, u] = a[t, u] - m[s, t] * a[s, u]
            if has_next:
                next_group = next_group - (next_cols[s] * inv[s]) * rows[s]
            for t in range(s + 1, 8):
                rows[t] = rows[t] - m[s, t] * rows[s]
                if has_next:
                    next_cols[t] = next_cols[t] - m[s, t] * next_cols[s]
        done[p] = out
        if p + 2 < 16:
            v = whole_parts(out)
            product = dot_t(left_of(v, 0), right_of(v, 0))
            for i in range(p + 2, 16):
                groups[i] = jnp.where(inside, 0.0, groups[i]) - product[8 * i:8 * i + 8, :]
        if has_next:
            groups[p + 1] = next_group
        hook(p)
    return jnp.concatenate(done, axis=0)


def factor_first(d_ref, li_ref):
    lane = lax.broadcasted_iota(jnp.int32, (8, 128), 1)
    sub = lax.broadcasted_iota(jnp.int32, (8, 128), 0)
    row = lax.broadcasted_iota(jnp.int32, (128, 128), 0)
    col = lax.broadcasted_iota(jnp.int32, (128, 128), 1)
    groups = [d_ref[8 * i:8 * i + 8, :] for i in range(16)]
    li_ref[...] = jnp.where(row >= col, factor_block(groups, lane, sub, lambda p: None), 0.0)


def factor_panel(a_ref, d_ref, xl_ref, xr_ref, li_ref, inv_ref, after):
    n, blocks = PANEL, PANEL // 128
    lane = lax.broadcasted_iota(jnp.int32, (8, 128), 1)
    sub = lax.broadcasted_iota(jnp.int32, (8, 128), 0)
    row = lax.broadcasted_iota(jnp.int32, (128, 128), 0)
    col = lax.broadcasted_iota(jnp.int32, (128, 128), 1)
    wide = lax.broadcasted_iota(jnp.int32, (128, n), 1)
    wide_row = lax.broadcasted_iota(jnp.int32, (128, n), 0)

    def rows_of(k):
        kb = pl.multiple_of(128 * k, 128)
        own = (wide >= kb) & (wide < kb + 128)
        r = jnp.where(own, jnp.where(wide - kb == wide_row, 1.0, 0.0), a_ref[pl.ds(kb, 128), :])
        v = dot6(li_ref[...], r)
        inv_ref[pl.ds(kb, 128), :] = jnp.where(wide < kb + 128, v, 0.0)
        return v

    def next_diagonal(k):
        kb = pl.multiple_of(128 * k, 128)
        nb = pl.multiple_of(128 * jnp.minimum(k + 1, blocks - 1), 128)
        v = parts(dot6(li_ref[...], a_ref[pl.ds(kb, 128), pl.ds(nb, 128)]))
        d_ref[...] = a_ref[pl.ds(nb, 128), pl.ds(nb, 128)] - dot_t(left_of(v, 0), right_of(v, 0))

    next_diagonal(0)

    def turn(k, carry):
        kb = pl.multiple_of(128 * k, 128)
        groups = [d_ref[8 * i:8 * i + 8, :] for i in range(16)]
        prev = k - 1
        pb = pl.multiple_of(128 * prev, 128)
        v = rows_of(prev)
        xl_ref[...] = left_of(parts(v.T), 1)
        xr_ref[...] = right_of(parts(v), 0)

        def hook(p):
            if not 1 <= p <= 8:
                return
            top, first = 128 + 448 * ((p - 1) % 2), 256 * ((p - 1) // 2)
            rows, cols = slice(top, top + 448), slice(first, first + 256)
            below = (top + lax.broadcasted_iota(jnp.int32, (448, 256), 0) >= kb)
            at_col = first + lax.broadcasted_iota(jnp.int32, (448, 256), 1)
            gone = (at_col >= pb) & (at_col < pb + 128)
            old = a_ref[rows, cols]
            new = jnp.where(gone, 0.0, old) - jnp.dot(
                xl_ref[rows, :], xr_ref[:, cols], preferred_element_type=F32
            )
            a_ref[rows, cols] = jnp.where(below, new, old)

        li_ref[...] = jnp.where(row >= col, factor_block(groups, lane, sub, hook), 0.0)
        next_diagonal(k)
        after(k)
        return carry

    lax.fori_loop(1, blocks, turn, 0)
    rows_of(blocks - 1)


def main_kernel(x_ref, gain_ref, damp_ref, hess_ref, fac_ref, upd_ref,
                xs, w, auxs, sx, sz, wn, xn, rms, wide, share, share_in, share_sum, share_y, g,
                slab, other, chip, far, a, d, xl, xr, li, inv, h12, final, extra, h1, hp, hq, u, corner, corner_in, corner_sum, corner_far, ss, rs):
    dp, z, h, x = spot()
    c, y = dp % 2, dp // 2
    column = [at(dp, (z + q // 2) % 4, (h + q % 2) % 2, x) for q in range(1, 8)]
    ring_x = [at(dp, z, h, (x + j) % 4) for j in range(1, 4)]
    ring_z = [at(dp, (z + j) % 4, h, x) for j in range(1, 4)]
    peer_c = at(y * 2 + 1 - c, z, h, x)
    peer_y = at((1 - y) * 2 + c, z, h, x)
    greet_signal(column + ring_x + [peer_c, peer_y])
    sent = []

    def copy(src, dst, i, dev, to=None):
        k = pltpu.make_async_remote_copy(src_ref=src, dst_ref=dst, send_sem=ss.at[i],
                                         recv_sem=rs.at[i if to is None else to],
                                         device_id=dev, device_id_type=MESH)
        return k

    def start(copies):
        for k in copies:
            k.start()
            sent.append(k)

    def arrive(copies):
        for k in copies:
            k.wait_recv()

    part = jnp.zeros((1024, 128), F32)
    for i in range(4):
        v = x_ref[:, 128 * i:128 * i + 128].astype(F32)
        part = part + v * v
    line = jnp.sum(part.T, axis=0, keepdims=True)
    for i in range(8):
        sx[x, i:i + 1, :] = line[:, 128 * i:128 * i + 128]
    is_source = (z == 0) & (h == 0)

    @pl.when(is_source)
    def _():
        own_damp = [v.astype(F32) for v in parts(damp_ref[...])]
        extra_rows = jnp.concatenate([gain_ref[...].astype(F32)] + own_damp + [jnp.zeros((12, 512), F32)], axis=0)
        for q in range(8):
            xs[q, 0:16, :] = extra_rows.astype(BF16)
            xs[q, 16:144, :] = x_ref[128 * q:128 * q + 128, :]
        w[x, 0] = xs[0]

    greet_wait(12)
    sum_x = [copy(sx.at[x], sx.at[x], 47 + j, ring_x[j]) for j in range(3)]
    start(sum_x)

    def scatter(q):
        return [copy(xs.at[q, pl.ds(p, n)], w.at[x, q, pl.ds(p, n)], 8 * i + q, column[q - 1], i)
                for i, (p, n) in enumerate([(0, 80), (80, 64)])]

    @pl.when(is_source)
    def _():
        for i in range(2):
            for q in range(1, 8):
                scatter(q)[i].start()

    own = z * 2 + h

    own_a, own_b = w.at[x, own, pl.ds(0, 80)], w.at[x, own, pl.ds(80, 64)]
    step_2b = [copy(own_b, own_b, 26 + q, column[q - 1]) for q in range(1, 8)]
    step_2a = [copy(own_a, own_a, 24 + j, ring_x[j]) for j in range(3)]
    def scattered(p, n, i):
        @pl.when(jnp.logical_not(is_source))
        def _():
            copy(xs.at[0, pl.ds(p, n)], w.at[x, own, pl.ds(p, n)], 0, column[0], i).wait_recv()

    scattered(0, 80, 0)
    start(step_2a)
    scattered(80, 64, 1)
    start(step_2b)
    arrive(sum_x)
    sz[own] = (sx[0] + sx[1]) + (sx[2] + sx[3])
    sum_c = [copy(sz.at[own], sz.at[own], 91 + q, column[q - 1]) for q in range(1, 8)]
    start(sum_c)
    all_a, all_b = w.at[:, own, pl.ds(16, 64)], w.at[x, :, pl.ds(80, 64)]
    step_3a = [copy(all_a, all_a, 36 + q, column[q - 1]) for q in range(1, 8)]
    step_3b = [copy(all_b, all_b, 44 + j, ring_x[j]) for j in range(3)]
    arrive(step_2a)
    start(step_3a)
    arrive(step_2b)
    start(step_3b)
    arrive(sum_c)

    total = ((sz[0] + sz[1]) + (sz[2] + sz[3])) + ((sz[4] + sz[5]) + (sz[6] + sz[7]))
    inverse = lax.rsqrt(total / D + 1e-05)
    for i in range(8):
        rms[128 * i:128 * i + 128, :] = jnp.broadcast_to(inverse[i:i + 1, :], (128, 128)).T

    @pl.loop(0, 8)
    def _(i):
        rows = pl.ds(pl.multiple_of(i * 128, 128), 128)
        scale = jnp.concatenate([rms[rows, :]] * 4, axis=1)
        xn[rows, :] = (x_ref[rows, :].astype(F32) * scale * gain_ref[...].astype(F32)).astype(BF16)

    for b in range(4):
        v = w[b, own, 0:16, :].astype(F32)
        auxs[b, 0:1, :] = v[0:1, :]
        auxs[b, 1:2, :] = (v[1:2, :] + v[2:3, :]) + v[3:4, :]
    arrive(step_3a)
    arrive(step_3b)

    def normalise(blocks):
        @pl.loop(0, 8)
        def _(i):
            rows = pl.ds(pl.multiple_of(i * 128, 128), 128)
            scale = jnp.concatenate([rms[rows, :]] * 4, axis=1)
            for b in blocks:
                wn[b, rows, :] = (w[b, i, 16:144, :].astype(F32) * scale * auxs[b, 0:1, :]).astype(BF16)

    s = z * 4 + x
    half = pl.ds(pl.multiple_of((s % 2) * 64, 64), 64)
    panels = [pl.ds(0, 1024), pl.ds(1024, 1024)]
    give, keep = pl.ds(pl.multiple_of(32 * (1 - c), 32), 32), pl.ds(pl.multiple_of(32 * c, 32), 32)

    def share_of(m):
        strip = wn[s // 8, :, pl.ds(pl.multiple_of(((s % 8) // 2) * 128, 128), 128)]
        for b in range(2):
            wide[:, 512 * b:512 * b + 512] = dot_t(strip, wn[2 * m + b]) * (1.0 / TOKENS)
        share[:, panels[m]] = wide[half, :]
        k = copy(share.at[give, panels[m]], share_in.at[:, panels[m]], 54 + 36 * m, peer_c)
        start([k])
        return k

    def slab_rows(b):
        slab[512 * b:512 * b + 512, :] = dot_t(wn[b], xn[...]) * (1.0 / TOKENS)

    normalise((0, 1))
    corner[...] = dot_t(wn[0, :, 0:128], wn[0, :, 0:128]) * (1.0 / TOKENS)
    corner_core = [copy(corner, corner_in, 99, peer_c)]
    start(corner_core)
    core_1 = share_of(0)
    normalise((2, 3))
    core_2 = share_of(1)
    slab_rows(0)
    slab_rows(1)
    spans = [(512 * (1 - c), 0, 512), (1024 + 256 * (1 - c), 512, 256), (1536 + 256 * (1 - c), 768, 256)]
    slabs = [
        copy(slab.at[pl.ds(pl.multiple_of(p, 256), n)], other.at[pl.ds(b, n)], 71 + i, peer_c)
        for i, (p, b, n) in enumerate(spans)
    ]
    slab_y = [copy(chip.at[pl.ds(p, 512)], far.at[pl.ds(p, 512)], 73 + i, peer_y)
              for i, p in ((1, 0), (18, 512))]
    start(slabs[:1])
    arrive([core_1])
    share_sum[:, panels[0]] = share[keep, panels[0]] + share_in[:, panels[0]]
    to_y = [copy(share_sum.at[:, panels[0]], share_y.at[:, pl.ds(0, 1024)], 55, peer_y)]
    start(to_y)
    arrive(corner_core)
    corner_sum[...] = corner[...] + corner_in[...]
    corner_y = [copy(corner_sum, corner_far, 100, peer_y)]
    start(corner_y)
    arrive([core_2])
    share_sum[:, panels[1]] = share[keep, panels[1]] + share_in[:, panels[1]]
    far_12 = pl.ds(pl.multiple_of(1024 + 512 * (1 - y), 512), 512)
    near_12 = pl.ds(pl.multiple_of(1024 + 512 * y, 512), 512)
    to_y2 = [copy(share_sum.at[:, far_12], share_y.at[:, pl.ds(1024, 512)], 56, peer_y)]
    start(to_y2)
    arrive(slabs[:1])
    chip[0:512, :] = slab[pl.ds(pl.multiple_of(512 * c, 512), 512), :] + other[0:512, :]
    start(slab_y[:1])
    arrive(to_y)
    g[z, x, c] = share_sum[:, 0:1024] + share_y[:, 0:1024]
    first, second = pl.ds(0, 16), pl.ds(16, 16)

    def gather_1(ref, i):
        one_a, one_b = ref.at[z, x, c, first], ref.at[z, x, c, second]
        return ([copy(one_a, one_a, i + j, ring_x[j]) for j in range(3)],
                [copy(one_b, one_b, i + 3 + j, ring_z[j]) for j in range(3)])

    def gather_2(ref, i):
        row_a, row_b = ref.at[z, :, c, first], ref.at[:, x, c, second]
        return ([copy(row_a, row_a, i + j, ring_z[j]) for j in range(3)],
                [copy(row_b, row_b, i + 3 + j, ring_x[j]) for j in range(3)])

    g1, g2 = gather_1(g, 57), gather_2(g, 63)
    g_core = [copy(g.at[:, :, c, k], g.at[:, :, c, k], i, peer_c) for k, i in ((first, 69), (second, 70))]
    q1, q2 = gather_1(h12, 75), gather_2(h12, 81)
    q_core = [copy(h12.at[:, :, c], h12.at[:, :, c], 87, peer_c)]
    start(g1[0] + g1[1])
    slab_rows(2)
    slab_rows(3)
    start(slabs[1:])
    row = lax.broadcasted_iota(jnp.int32, (128, 128), 0)
    col = lax.broadcasted_iota(jnp.int32, (128, 128), 1)
    arrive(g1[0])
    start(g2[0])
    arrive(g1[1])
    start(g2[1])
    arrive(to_y2)
    h12[z, x, c] = share_sum[:, near_12] + share_y[:, 1024:1536]
    arrive(slabs[1:])
    chip[512:768, :] = slab[pl.ds(pl.multiple_of(1024 + 256 * c, 256), 256), :] + other[512:768, :]
    chip[768:1024, :] = slab[pl.ds(pl.multiple_of(1536 + 256 * c, 256), 256), :] + other[768:1024, :]
    start(slab_y[1:])
    arrive(corner_y)
    d[...] = corner_sum[...] + corner_far[...] + jnp.where(row == col, auxs[0, 1:2, 0:128], 0.0)
    factor_first(d, li)
    arrive(g2[0])
    start(g_core[:1])
    arrive(g2[1])
    start(g_core[1:])
    start(q1[0] + q1[1])
    arrive(g_core)
    for i in range(4):
        for j in range(4):
            for k in range(2):
                lo = 64 * (4 * i + j) + 32 * k
                a[lo:lo + 32, :] = g[i, j, k]
    for k in range(8):
        at_k = slice(128 * k, 128 * k + 128)
        damp = auxs[k // 4, 1:2, 128 * (k % 4):128 * (k % 4) + 128]
        a[at_k, at_k] = a[at_k, at_k] + jnp.where(row == col, damp, 0.0)

    block = pl.multiple_of(512 + 256 * (1 - c), 256)
    to_e = [copy(final.at[pl.ds(0, 512)], extra.at[pl.ds(0, 512)], 88, peer_c),
            copy(final.at[pl.ds(block, 256)], extra.at[pl.ds(512, 256)], 89, peer_c)]

    def after(k):
        @pl.when(k == 1)
        def _():
            arrive(q1[0])
            arrive(q1[1])
            for m in q2[0] + q2[1]:
                m.start()

        @pl.when(k == 4)
        def _():
            arrive(q2[0])
            arrive(q2[1])
            for m in q_core:
                m.start()

        @pl.when(k == 6)
        def _():
            arrive(slab_y)
            final[...] = chip[...] + far[...]
            for m in to_e:
                m.start()

    factor_panel(a, d, xl, xr, li, inv, after)
    arrive(q_core + to_e)

    first_col = (z * 8 + h * 4 + x) * 512
    damp_own = damp_ref[...]

    def damped(value, first_row):
        rows = first_row + lax.broadcasted_iota(jnp.int32, value.shape, 0)
        cols = first_col + lax.broadcasted_iota(jnp.int32, value.shape, 1)
        return value + jnp.where(rows == cols, damp_own, 0.0)

    mine = pl.multiple_of(512 * c, 512)
    theirs = pl.multiple_of(512 * (1 - c), 512)
    h1[pl.ds(mine, 512), :] = damped(final[0:512, :], mine)
    h1[pl.ds(theirs, 512), :] = damped(extra[0:512, :], theirs)

    @pl.when(y == 0)
    def _():
        hess_ref[...] = h1[pl.ds(mine, 512), :]

    @pl.when(y == 1)
    def _():
        p = pl.multiple_of(256 * c, 256)
        q = pl.multiple_of(256 * (1 - c), 256)
        hess_ref[pl.ds(p, 256), :] = damped(final[pl.ds(512 + p, 256), :], 1024 + 512 * c + p)
        hess_ref[pl.ds(q, 256), :] = damped(extra[512:768, :], 1024 + 512 * c + q)

    for i in range(8):
        rows = slice(128 * i, 128 * i + 128)
        hp[rows, 0:512], hq[rows, 0:512] = two_parts(h1[rows, :])
        for j in range(2):
            p = 128 * i + 64 * j
            block12 = jnp.concatenate(
                [h12[i // 2, 2 * (i % 2) + j, m, :, pl.ds(pl.multiple_of(256 * c, 256), 256)] for m in range(2)], axis=0
            )
            hp[p:p + 64, 512:768], hq[p:p + 64, 512:768] = two_parts(block12)
    for i in range(2):
        rows, n = slice(512 * i, 512 * i + 512), 512 * i + 512
        p, q = two_parts(inv[rows, 0:n])
        u[rows, :] = jnp.dot(
            jnp.concatenate([p, p, q], axis=1),
            jnp.concatenate([hp[0:n, :], hq[0:n, :], hp[0:n, :]], axis=0),
            preferred_element_type=F32,
        )
    fac_ref[...] = u[pl.ds(pl.multiple_of(256 * dp, 256), 256), 0:512]
    p, q = two_parts(u[:, 512:768])
    v, r = two_parts(u[:, 0:512])
    upd_ref[...] = damped(
        final[pl.ds(pl.multiple_of(512 + 256 * y, 256), 256), :], 1024 + 256 * dp
    ) - dot_t(jnp.concatenate([p, p, q], axis=0), jnp.concatenate([v, r, v], axis=0))
    for k in sent + q2[0] + q2[1] + q_core + to_e:
        k.wait_send()

    @pl.when(is_source)
    def _():
        for q in range(1, 8):
            for k in scatter(q):
                k.wait_send()


def main(hidden, gain, damping):
    def f32(*shape):
        return pltpu.VMEM(shape, F32)

    def b16(*shape):
        return pltpu.VMEM(shape, BF16)

    return pl.pallas_call(
        main_kernel,
        out_shape=(
            jax.ShapeDtypeStruct((512, 512), F32),
            jax.ShapeDtypeStruct((256, 512), F32),
            jax.ShapeDtypeStruct((256, 512), F32),
        ),
        in_specs=[VM, VM, VM],
        out_specs=(VM, VM, VM),
        scratch_shapes=[
            b16(8, 144, 512), b16(4, 8, 144, 512), f32(4, 8, 512), f32(4, 8, 128), f32(8, 8, 128),
            b16(4, 1024, 512), b16(1024, 512), f32(1024, 128), f32(128, 1024), f32(64, 2048),
            f32(32, 2048), f32(32, 2048), f32(32, 1536), f32(4, 4, 2, 32, 1024),
            f32(2048, 512), f32(1024, 512), f32(1024, 512), f32(1024, 512),
            f32(PANEL, PANEL), f32(128, 128), b16(PANEL, 768), b16(768, PANEL), f32(128, 128),
            f32(PANEL, PANEL), f32(4, 4, 2, 32, 512), f32(1024, 512), f32(768, 512),
            f32(1024, 512), b16(1024, 768), b16(1024, 768), f32(1024, 768),
            f32(128, 128), f32(128, 128), f32(128, 128), f32(128, 128),
            pltpu.SemaphoreType.DMA((101,)),
            pltpu.SemaphoreType.DMA((101,)),
        ],
        compiler_params=params(collective_id=0, has_side_effects=True),
        name="window_panel",
    )(hidden, gain, damping)


def body(hidden_states, norm_gain, damping):
    return main(hidden_states, norm_gain[None], damping[None])


def solution(mesh):
    return jax.shard_map(
        body,
        mesh=mesh,
        in_specs=(P("dp", "mp"), P("mp"), P("mp")),
        out_specs=(P("dp", "mp"), P("dp", "mp"), P("dp", "mp")),
        check_vma=False,
    )
```

```python
import jax
import jax.numpy as jnp
from jax import lax
from jax.experimental import pallas as pl
from jax.experimental.pallas import tpu as pltpu
from jax.sharding import PartitionSpec as P

D = 16384
PANEL = 1024
TOKENS = 4096
MESH = pl.DeviceIdType.MESH
F32 = jnp.float32
BF16 = jnp.bfloat16
VM = pl.BlockSpec(memory_space=pltpu.VMEM)


def params(**kw):
    return pltpu.CompilerParams(vmem_limit_bytes=60 * 2**20, **kw)


def spot():
    mp = lax.axis_index("mp")
    return lax.axis_index("dp"), mp // 8, (mp // 4) % 2, mp % 4


def at(dp, z, h, x):
    return (dp, z * 8 + h * 4 + x)


def greet_signal(partners):
    barrier = pltpu.get_barrier_semaphore()
    for p in partners:
        pl.semaphore_signal(barrier, inc=1, device_id=p, device_id_type=MESH)


def greet_wait(count):
    pl.semaphore_wait(pltpu.get_barrier_semaphore(), count)


def dot_t(a, b):
    return lax.dot_general(a, b, (((0,), (0,)), ((), ())), preferred_element_type=F32)


def parts(v):
    a = v.astype(BF16)
    r = v - a.astype(F32)
    b = r.astype(BF16)
    return a, b, (r - b.astype(F32)).astype(BF16)


def whole_parts(v):
    v = jnp.concatenate([v, jnp.zeros_like(v)], axis=0)
    return parts(v)


def left_of(p, axis):
    a, b, c = p
    return jnp.concatenate([a, a, a, b, b, c], axis=axis)


def right_of(p, axis):
    a, b, c = p
    return jnp.concatenate([a, b, c, a, b, a], axis=axis)


def two_parts(v):
    a = v.astype(BF16)
    return a, (v - a.astype(F32)).astype(BF16)


def dot6(a, b):
    return jnp.dot(left_of(parts(a), 1), right_of(parts(b), 0), preferred_element_type=F32)


def lane_of(v, j):
    return jnp.broadcast_to(v[:, j:j + 1], (8, 128))


def row_of(v, r):
    return jnp.broadcast_to(v[r:r + 1, :], (8, 128))


def factor_block(groups, lane, sub, hook):
    done = [None] * 16
    groups = list(groups)
    for p in range(16):
        base = 8 * p
        here = groups[p]
        inside = (lane >= base) & (lane < base + 8)
        cols = [lane_of(here, base + t) for t in range(8)]
        a = {(r, t): row_of(cols[t], r) for t in range(8) for r in range(t + 1)}
        opened = jnp.where(inside, jnp.where(lane - base == sub, 1.0, 0.0), here)
        rows = [row_of(opened, r) for r in range(8)]
        has_next = p + 1 < 16
        if has_next:
            next_cols = [lane_of(groups[p + 1], base + t) for t in range(8)]
            next_group = jnp.where(inside, 0.0, groups[p + 1])
        m, inv = {}, {}
        out = jnp.zeros((8, 128), F32)
        for s in range(8):
            inv[s] = 1.0 / a[s, s]
            out = jnp.where(sub == s, rows[s] * lax.rsqrt(a[s, s]), out)
            for t in range(s + 1, 8):
                m[s, t] = a[s, t] * inv[s]
                for u in range(t, 8):
                    a[t, u] = a[t, u] - m[s, t] * a[s, u]
            if has_next:
                next_group = next_group - (next_cols[s] * inv[s]) * rows[s]
            for t in range(s + 1, 8):
                rows[t] = rows[t] - m[s, t] * rows[s]
                if has_next:
                    next_cols[t] = next_cols[t] - m[s, t] * next_cols[s]
        done[p] = out
        if p + 2 < 16:
            v = whole_parts(out)
            product = dot_t(left_of(v, 0), right_of(v, 0))
            for i in range(p + 2, 16):
                groups[i] = jnp.where(inside, 0.0, groups[i]) - product[8 * i:8 * i + 8, :]
        if has_next:
            groups[p + 1] = next_group
        hook(p)
    return jnp.concatenate(done, axis=0)


def factor_first(d_ref, li_ref):
    lane = lax.broadcasted_iota(jnp.int32, (8, 128), 1)
    sub = lax.broadcasted_iota(jnp.int32, (8, 128), 0)
    row = lax.broadcasted_iota(jnp.int32, (128, 128), 0)
    col = lax.broadcasted_iota(jnp.int32, (128, 128), 1)
    groups = [d_ref[8 * i:8 * i + 8, :] for i in range(16)]
    li_ref[...] = jnp.where(row >= col, factor_block(groups, lane, sub, lambda p: None), 0.0)


def factor_panel(a_ref, d_ref, xl_ref, xr_ref, li_ref, inv_ref, after):
    n, blocks = PANEL, PANEL // 128
    lane = lax.broadcasted_iota(jnp.int32, (8, 128), 1)
    sub = lax.broadcasted_iota(jnp.int32, (8, 128), 0)
    row = lax.broadcasted_iota(jnp.int32, (128, 128), 0)
    col = lax.broadcasted_iota(jnp.int32, (128, 128), 1)
    wide = lax.broadcasted_iota(jnp.int32, (128, n), 1)
    wide_row = lax.broadcasted_iota(jnp.int32, (128, n), 0)

    def rows_of(k):
        kb = pl.multiple_of(128 * k, 128)
        own = (wide >= kb) & (wide < kb + 128)
        r = jnp.where(own, jnp.where(wide - kb == wide_row, 1.0, 0.0), a_ref[pl.ds(kb, 128), :])
        v = dot6(li_ref[...], r)
        inv_ref[pl.ds(kb, 128), :] = jnp.where(wide < kb + 128, v, 0.0)
        return v

    def next_diagonal(k):
        kb = pl.multiple_of(128 * k, 128)
        nb = pl.multiple_of(128 * jnp.minimum(k + 1, blocks - 1), 128)
        v = parts(dot6(li_ref[...], a_ref[pl.ds(kb, 128), pl.ds(nb, 128)]))
        d_ref[...] = a_ref[pl.ds(nb, 128), pl.ds(nb, 128)] - dot_t(left_of(v, 0), right_of(v, 0))

    next_diagonal(0)

    def turn(k, carry):
        kb = pl.multiple_of(128 * k, 128)
        groups = [d_ref[8 * i:8 * i + 8, :] for i in range(16)]
        prev = k - 1
        pb = pl.multiple_of(128 * prev, 128)
        v = rows_of(prev)
        xl_ref[...] = left_of(parts(v.T), 1)
        xr_ref[...] = right_of(parts(v), 0)

        def hook(p):
            if not 1 <= p <= 8:
                return
            top, first = 128 + 448 * ((p - 1) % 2), 256 * ((p - 1) // 2)
            rows, cols = slice(top, top + 448), slice(first, first + 256)
            below = (top + lax.broadcasted_iota(jnp.int32, (448, 256), 0) >= kb)
            at_col = first + lax.broadcasted_iota(jnp.int32, (448, 256), 1)
            gone = (at_col >= pb) & (at_col < pb + 128)
            old = a_ref[rows, cols]
            new = jnp.where(gone, 0.0, old) - jnp.dot(
                xl_ref[rows, :], xr_ref[:, cols], preferred_element_type=F32
            )
            a_ref[rows, cols] = jnp.where(below, new, old)

        li_ref[...] = jnp.where(row >= col, factor_block(groups, lane, sub, hook), 0.0)
        next_diagonal(k)
        after(k)
        return carry

    lax.fori_loop(1, blocks, turn, 0)
    rows_of(blocks - 1)


def main_kernel(x_ref, gain_ref, damp_ref, hess_ref, fac_ref, upd_ref,
                xs, w, auxs, sx, sz, wn, xn, rms, wide, share, share_in, share_sum, share_y, g,
                slab, other, chip, far, a, d, xl, xr, li, inv, h12, final, extra, h1, hp, hq, u, corner, corner_in, corner_sum, corner_far, ss, rs):
    dp, z, h, x = spot()
    c, y = dp % 2, dp // 2
    column = [at(dp, (z + q // 2) % 4, (h + q % 2) % 2, x) for q in range(1, 8)]
    ring_x = [at(dp, z, h, (x + j) % 4) for j in range(1, 4)]
    ring_z = [at(dp, (z + j) % 4, h, x) for j in range(1, 4)]
    peer_c = at(y * 2 + 1 - c, z, h, x)
    peer_y = at((1 - y) * 2 + c, z, h, x)
    greet_signal(column + ring_x + [peer_c, peer_y])
    sent = []

    def copy(src, dst, i, dev, to=None):
        k = pltpu.make_async_remote_copy(src_ref=src, dst_ref=dst, send_sem=ss.at[i],
                                         recv_sem=rs.at[i if to is None else to],
                                         device_id=dev, device_id_type=MESH)
        return k

    def start(copies):
        for k in copies:
            k.start()
            sent.append(k)

    def arrive(copies):
        for k in copies:
            k.wait_recv()

    part = jnp.zeros((1024, 128), F32)
    for i in range(4):
        v = x_ref[:, 128 * i:128 * i + 128].astype(F32)
        part = part + v * v
    line = jnp.sum(part.T, axis=0, keepdims=True)
    for i in range(8):
        sx[x, i:i + 1, :] = line[:, 128 * i:128 * i + 128]
    is_source = (z == 0) & (h == 0)

    @pl.when(is_source)
    def _():
        own_damp = [v.astype(F32) for v in parts(damp_ref[...])]
        extra_rows = jnp.concatenate([gain_ref[...].astype(F32)] + own_damp + [jnp.zeros((12, 512), F32)], axis=0)
        for q in range(8):
            xs[q, 0:16, :] = extra_rows.astype(BF16)
            xs[q, 16:144, :] = x_ref[128 * q:128 * q + 128, :]
        w[x, 0, 0] = xs[0]

    greet_wait(12)
    sum_x = [copy(sx.at[x], sx.at[x], 47 + j, ring_x[j]) for j in range(3)]
    start(sum_x)

    def scatter(q):
        return [copy(xs.at[q, pl.ds(p, n)], w.at[x, q // 2, q % 2, pl.ds(p, n)], 8 * i + q, column[q - 1], i)
                for i, (p, n) in enumerate([(0, 96), (96, 48)])]

    @pl.when(is_source)
    def _():
        for i in range(2):
            for q in range(1, 8):
                scatter(q)[i].start()

    own = z * 2 + h

    arrive(sum_x)
    sz[own] = (sx[0] + sx[1]) + (sx[2] + sx[3])
    sum_c = [copy(sz.at[own], sz.at[own], 91 + q, column[q - 1]) for q in range(1, 8)]
    start(sum_c)

    own_a, own_b = w.at[x, z, h, pl.ds(0, 96)], w.at[x, z, h, pl.ds(96, 48)]
    step_2b = [copy(own_b, own_b, 26 + q, column[q - 1]) for q in range(1, 8)]
    step_2a = [copy(own_a, own_a, 24 + j, ring_x[j]) for j in range(3)]
    def scattered(p, n, i):
        @pl.when(jnp.logical_not(is_source))
        def _():
            copy(xs.at[0, pl.ds(p, n)], w.at[x, z, h, pl.ds(p, n)], 0, column[0], i).wait_recv()

    scattered(0, 96, 0)
    start(step_2a)
    scattered(96, 48, 1)
    start(step_2b)
    all_b = w.at[x, :, :, pl.ds(96, 48)]
    over_z, over_h = w.at[:, z, h, pl.ds(16, 48)], w.at[:, z, h, pl.ds(64, 32)]
    then_h, then_z = w.at[:, :, h, pl.ds(16, 48)], w.at[:, z, :, pl.ds(64, 32)]
    peer_h = at(dp, z, 1 - h, x)
    step_3z = [copy(over_z, over_z, 36 + j, ring_z[j]) for j in range(3)]
    step_3h = [copy(over_h, over_h, 39, peer_h)]
    step_4h = [copy(then_h, then_h, 40, peer_h)]
    step_4z = [copy(then_z, then_z, 41 + j, ring_z[j]) for j in range(3)]
    step_3b = [copy(all_b, all_b, 44 + j, ring_x[j]) for j in range(3)]
    arrive(step_2a)
    start(step_3z + step_3h)
    arrive(step_2b)
    start(step_3b)
    arrive(step_3h)
    start(step_4z)
    arrive(step_3z)
    start(step_4h)
    arrive(sum_c)

    total = ((sz[0] + sz[1]) + (sz[2] + sz[3])) + ((sz[4] + sz[5]) + (sz[6] + sz[7]))
    inverse = lax.rsqrt(total / D + 1e-05)
    for i in range(8):
        rms[128 * i:128 * i + 128, :] = jnp.broadcast_to(inverse[i:i + 1, :], (128, 128)).T

    @pl.loop(0, 8)
    def _(i):
        rows = pl.ds(pl.multiple_of(i * 128, 128), 128)
        scale = jnp.concatenate([rms[rows, :]] * 4, axis=1)
        xn[rows, :] = (x_ref[rows, :].astype(F32) * scale * gain_ref[...].astype(F32)).astype(BF16)

    for b in range(4):
        v = w[b, z, h, 0:16, :].astype(F32)
        auxs[b, 0:1, :] = v[0:1, :]
        auxs[b, 1:2, :] = (v[1:2, :] + v[2:3, :]) + v[3:4, :]
    arrive(step_4z + step_4h)
    arrive(step_3b)

    def normalise(blocks):
        @pl.loop(0, 8)
        def _(i):
            rows = pl.ds(pl.multiple_of(i * 128, 128), 128)
            scale = jnp.concatenate([rms[rows, :]] * 4, axis=1)
            for b in blocks:
                wn[b, rows, :] = (w[b, i // 2, i % 2, 16:144, :].astype(F32) * scale * auxs[b, 0:1, :]).astype(BF16)

    s = z * 4 + x
    half = pl.ds(pl.multiple_of((s % 2) * 64, 64), 64)
    panels = [pl.ds(0, 1024), pl.ds(1024, 1024)]
    give, keep = pl.ds(pl.multiple_of(32 * (1 - c), 32), 32), pl.ds(pl.multiple_of(32 * c, 32), 32)

    def share_of(m):
        strip = wn[s // 8, :, pl.ds(pl.multiple_of(((s % 8) // 2) * 128, 128), 128)]
        for b in range(2):
            wide[:, 512 * b:512 * b + 512] = dot_t(strip, wn[2 * m + b]) * (1.0 / TOKENS)
        share[:, panels[m]] = wide[half, :]
        k = copy(share.at[give, panels[m]], share_in.at[:, panels[m]], 54 + 36 * m, peer_c)
        start([k])
        return k

    def slab_rows(b):
        slab[512 * b:512 * b + 512, :] = dot_t(wn[b], xn[...]) * (1.0 / TOKENS)

    normalise((0, 1))
    corner[...] = dot_t(wn[0, :, 0:128], wn[0, :, 0:128]) * (1.0 / TOKENS)
    corner_core = [copy(corner, corner_in, 99, peer_c)]
    start(corner_core)
    core_1 = share_of(0)
    normalise((2, 3))
    core_2 = share_of(1)
    slab_rows(0)
    slab_rows(1)
    spans = [(512 * (1 - c), 0, 512), (1024 + 256 * (1 - c), 512, 256), (1536 + 256 * (1 - c), 768, 256)]
    slabs = [
        copy(slab.at[pl.ds(pl.multiple_of(p, 256), n)], other.at[pl.ds(b, n)], 71 + i, peer_c)
        for i, (p, b, n) in enumerate(spans)
    ]
    slab_y = [copy(chip.at[pl.ds(p, 512)], far.at[pl.ds(p, 512)], 73 + i, peer_y)
              for i, p in ((1, 0), (18, 512))]
    start(slabs[:1])
    arrive([core_1])
    share_sum[:, panels[0]] = share[keep, panels[0]] + share_in[:, panels[0]]
    to_y = [copy(share_sum.at[:, panels[0]], share_y.at[:, pl.ds(0, 1024)], 55, peer_y)]
    start(to_y)
    arrive(corner_core)
    corner_sum[...] = corner[...] + corner_in[...]
    corner_y = [copy(corner_sum, corner_far, 100, peer_y)]
    start(corner_y)
    arrive([core_2])
    share_sum[:, panels[1]] = share[keep, panels[1]] + share_in[:, panels[1]]
    far_12 = pl.ds(pl.multiple_of(1024 + 512 * (1 - y), 512), 512)
    near_12 = pl.ds(pl.multiple_of(1024 + 512 * y, 512), 512)
    to_y2 = [copy(share_sum.at[:, far_12], share_y.at[:, pl.ds(1024, 512)], 56, peer_y)]
    start(to_y2)
    arrive(slabs[:1])
    chip[0:512, :] = slab[pl.ds(pl.multiple_of(512 * c, 512), 512), :] + other[0:512, :]
    start(slab_y[:1])
    arrive(to_y)
    g[z, x, c] = share_sum[:, 0:1024] + share_y[:, 0:1024]
    first, second = pl.ds(0, 16), pl.ds(16, 16)

    def gather_1(ref, i):
        one_a, one_b = ref.at[z, x, c, first], ref.at[z, x, c, second]
        return ([copy(one_a, one_a, i + j, ring_x[j]) for j in range(3)],
                [copy(one_b, one_b, i + 3 + j, ring_z[j]) for j in range(3)])

    def gather_2(ref, i):
        row_a, row_b = ref.at[z, :, c, first], ref.at[:, x, c, second]
        return ([copy(row_a, row_a, i + j, ring_z[j]) for j in range(3)],
                [copy(row_b, row_b, i + 3 + j, ring_x[j]) for j in range(3)])

    g1, g2 = gather_1(g, 57), gather_2(g, 63)
    g_core = [copy(g.at[:, :, c, k], g.at[:, :, c, k], i, peer_c) for k, i in ((first, 69), (second, 70))]
    q1, q2 = gather_1(h12, 75), gather_2(h12, 81)
    q_core = [copy(h12.at[:, :, c], h12.at[:, :, c], 87, peer_c)]
    start(g1[0] + g1[1])
    slab_rows(2)
    slab_rows(3)
    start(slabs[1:])
    row = lax.broadcasted_iota(jnp.int32, (128, 128), 0)
    col = lax.broadcasted_iota(jnp.int32, (128, 128), 1)
    arrive(g1[0])
    start(g2[0])
    arrive(g1[1])
    start(g2[1])
    arrive(to_y2)
    h12[z, x, c] = share_sum[:, near_12] + share_y[:, 1024:1536]
    arrive(slabs[1:])
    chip[512:768, :] = slab[pl.ds(pl.multiple_of(1024 + 256 * c, 256), 256), :] + other[512:768, :]
    chip[768:1024, :] = slab[pl.ds(pl.multiple_of(1536 + 256 * c, 256), 256), :] + other[768:1024, :]
    start(slab_y[1:])
    arrive(corner_y)
    d[...] = corner_sum[...] + corner_far[...] + jnp.where(row == col, auxs[0, 1:2, 0:128], 0.0)
    factor_first(d, li)
    arrive(g2[0])
    start(g_core[:1])
    arrive(g2[1])
    start(g_core[1:])
    start(q1[0] + q1[1])
    arrive(g_core)
    for i in range(4):
        for j in range(4):
            for k in range(2):
                lo = 64 * (4 * i + j) + 32 * k
                a[lo:lo + 32, :] = g[i, j, k]
    for k in range(8):
        at_k = slice(128 * k, 128 * k + 128)
        damp = auxs[k // 4, 1:2, 128 * (k % 4):128 * (k % 4) + 128]
        a[at_k, at_k] = a[at_k, at_k] + jnp.where(row == col, damp, 0.0)

    block = pl.multiple_of(512 + 256 * (1 - c), 256)
    to_e = [copy(final.at[pl.ds(0, 512)], extra.at[pl.ds(0, 512)], 88, peer_c),
            copy(final.at[pl.ds(block, 256)], extra.at[pl.ds(512, 256)], 89, peer_c)]

    def after(k):
        @pl.when(k == 1)
        def _():
            arrive(q1[0])
            arrive(q1[1])
            for m in q2[0] + q2[1]:
                m.start()

        @pl.when(k == 4)
        def _():
            arrive(q2[0])
            arrive(q2[1])
            for m in q_core:
                m.start()

        @pl.when(k == 6)
        def _():
            arrive(slab_y)
            final[...] = chip[...] + far[...]
            for m in to_e:
                m.start()

    factor_panel(a, d, xl, xr, li, inv, after)
    arrive(q_core + to_e)

    first_col = (z * 8 + h * 4 + x) * 512
    damp_own = damp_ref[...]

    def damped(value, first_row):
        rows = first_row + lax.broadcasted_iota(jnp.int32, value.shape, 0)
        cols = first_col + lax.broadcasted_iota(jnp.int32, value.shape, 1)
        return value + jnp.where(rows == cols, damp_own, 0.0)

    mine = pl.multiple_of(512 * c, 512)
    theirs = pl.multiple_of(512 * (1 - c), 512)
    h1[pl.ds(mine, 512), :] = damped(final[0:512, :], mine)
    h1[pl.ds(theirs, 512), :] = damped(extra[0:512, :], theirs)

    @pl.when(y == 0)
    def _():
        hess_ref[...] = h1[pl.ds(mine, 512), :]

    @pl.when(y == 1)
    def _():
        p = pl.multiple_of(256 * c, 256)
        q = pl.multiple_of(256 * (1 - c), 256)
        hess_ref[pl.ds(p, 256), :] = damped(final[pl.ds(512 + p, 256), :], 1024 + 512 * c + p)
        hess_ref[pl.ds(q, 256), :] = damped(extra[512:768, :], 1024 + 512 * c + q)

    for i in range(8):
        rows = slice(128 * i, 128 * i + 128)
        hp[rows, 0:512], hq[rows, 0:512] = two_parts(h1[rows, :])
        for j in range(2):
            p = 128 * i + 64 * j
            block12 = jnp.concatenate(
                [h12[i // 2, 2 * (i % 2) + j, m, :, pl.ds(pl.multiple_of(256 * c, 256), 256)] for m in range(2)], axis=0
            )
            hp[p:p + 64, 512:768], hq[p:p + 64, 512:768] = two_parts(block12)
    for i in range(2):
        rows, n = slice(512 * i, 512 * i + 512), 512 * i + 512
        p, q = two_parts(inv[rows, 0:n])
        u[rows, :] = jnp.dot(
            jnp.concatenate([p, p, q], axis=1),
            jnp.concatenate([hp[0:n, :], hq[0:n, :], hp[0:n, :]], axis=0),
            preferred_element_type=F32,
        )
    fac_ref[...] = u[pl.ds(pl.multiple_of(256 * dp, 256), 256), 0:512]
    p, q = two_parts(u[:, 512:768])
    v, r = two_parts(u[:, 0:512])
    upd_ref[...] = damped(
        final[pl.ds(pl.multiple_of(512 + 256 * y, 256), 256), :], 1024 + 256 * dp
    ) - dot_t(jnp.concatenate([p, p, q], axis=0), jnp.concatenate([v, r, v], axis=0))
    for k in sent + q2[0] + q2[1] + q_core + to_e:
        k.wait_send()

    @pl.when(is_source)
    def _():
        for q in range(1, 8):
            for k in scatter(q):
                k.wait_send()


def main(hidden, gain, damping):
    def f32(*shape):
        return pltpu.VMEM(shape, F32)

    def b16(*shape):
        return pltpu.VMEM(shape, BF16)

    return pl.pallas_call(
        main_kernel,
        out_shape=(
            jax.ShapeDtypeStruct((512, 512), F32),
            jax.ShapeDtypeStruct((256, 512), F32),
            jax.ShapeDtypeStruct((256, 512), F32),
        ),
        in_specs=[VM, VM, VM],
        out_specs=(VM, VM, VM),
        scratch_shapes=[
            b16(8, 144, 512), b16(4, 4, 2, 144, 512), f32(4, 8, 512), f32(4, 8, 128), f32(8, 8, 128),
            b16(4, 1024, 512), b16(1024, 512), f32(1024, 128), f32(128, 1024), f32(64, 2048),
            f32(32, 2048), f32(32, 2048), f32(32, 1536), f32(4, 4, 2, 32, 1024),
            f32(2048, 512), f32(1024, 512), f32(1024, 512), f32(1024, 512),
            f32(PANEL, PANEL), f32(128, 128), b16(PANEL, 768), b16(768, PANEL), f32(128, 128),
            f32(PANEL, PANEL), f32(4, 4, 2, 32, 512), f32(1024, 512), f32(768, 512),
            f32(1024, 512), b16(1024, 768), b16(1024, 768), f32(1024, 768),
            f32(128, 128), f32(128, 128), f32(128, 128), f32(128, 128),
            pltpu.SemaphoreType.DMA((101,)),
            pltpu.SemaphoreType.DMA((101,)),
        ],
        compiler_params=params(collective_id=0, has_side_effects=True),
        name="window_panel",
    )(hidden, gain, damping)


def body(hidden_states, norm_gain, damping):
    return main(hidden_states, norm_gain[None], damping[None])


def solution(mesh):
    return jax.shard_map(
        body,
        mesh=mesh,
        in_specs=(P("dp", "mp"), P("mp"), P("mp")),
        out_specs=(P("dp", "mp"), P("dp", "mp"), P("dp", "mp")),
        check_vma=False,
    )
```

```python
import jax
import jax.numpy as jnp
from jax import lax
from jax.experimental import pallas as pl
from jax.experimental.pallas import tpu as pltpu
from jax.sharding import PartitionSpec as P

D = 16384
PANEL = 1024
TOKENS = 4096
MESH = pl.DeviceIdType.MESH
F32 = jnp.float32
BF16 = jnp.bfloat16
VM = pl.BlockSpec(memory_space=pltpu.VMEM)


def params(**kw):
    return pltpu.CompilerParams(vmem_limit_bytes=60 * 2**20, **kw)


def spot():
    mp = lax.axis_index("mp")
    return lax.axis_index("dp"), mp // 8, (mp // 4) % 2, mp % 4


def at(dp, z, h, x):
    return (dp, z * 8 + h * 4 + x)


def greet_signal(partners):
    barrier = pltpu.get_barrier_semaphore()
    for p in partners:
        pl.semaphore_signal(barrier, inc=1, device_id=p, device_id_type=MESH)


def greet_wait(count):
    pl.semaphore_wait(pltpu.get_barrier_semaphore(), count)


def dot_t(a, b):
    return lax.dot_general(a, b, (((0,), (0,)), ((), ())), preferred_element_type=F32)


def parts(v):
    a = v.astype(BF16)
    r = v - a.astype(F32)
    b = r.astype(BF16)
    return a, b, (r - b.astype(F32)).astype(BF16)


def whole_parts(v):
    v = jnp.concatenate([v, jnp.zeros_like(v)], axis=0)
    return parts(v)


def left_of(p, axis):
    a, b, c = p
    return jnp.concatenate([a, a, a, b, b, c], axis=axis)


def right_of(p, axis):
    a, b, c = p
    return jnp.concatenate([a, b, c, a, b, a], axis=axis)


def two_parts(v):
    a = v.astype(BF16)
    return a, (v - a.astype(F32)).astype(BF16)


def dot6(a, b):
    return jnp.dot(left_of(parts(a), 1), right_of(parts(b), 0), preferred_element_type=F32)


def lane_of(v, j):
    return jnp.broadcast_to(v[:, j:j + 1], (8, 128))


def row_of(v, r):
    return jnp.broadcast_to(v[r:r + 1, :], (8, 128))


def factor_block(groups, lane, sub, hook):
    done = [None] * 16
    groups = list(groups)
    for p in range(16):
        base = 8 * p
        here = groups[p]
        inside = (lane >= base) & (lane < base + 8)
        cols = [lane_of(here, base + t) for t in range(8)]
        a = {(r, t): row_of(cols[t], r) for t in range(8) for r in range(t + 1)}
        opened = jnp.where(inside, jnp.where(lane - base == sub, 1.0, 0.0), here)
        rows = [row_of(opened, r) for r in range(8)]
        has_next = p + 1 < 16
        if has_next:
            next_cols = [lane_of(groups[p + 1], base + t) for t in range(8)]
            next_group = jnp.where(inside, 0.0, groups[p + 1])
        m, inv = {}, {}
        out = jnp.zeros((8, 128), F32)
        for s in range(8):
            inv[s] = 1.0 / a[s, s]
            out = jnp.where(sub == s, rows[s] * lax.rsqrt(a[s, s]), out)
            for t in range(s + 1, 8):
                m[s, t] = a[s, t] * inv[s]
                for u in range(t, 8):
                    a[t, u] = a[t, u] - m[s, t] * a[s, u]
            if has_next:
                next_group = next_group - (next_cols[s] * inv[s]) * rows[s]
            for t in range(s + 1, 8):
                rows[t] = rows[t] - m[s, t] * rows[s]
                if has_next:
                    next_cols[t] = next_cols[t] - m[s, t] * next_cols[s]
        done[p] = out
        if p + 2 < 16:
            v = whole_parts(out)
            product = dot_t(left_of(v, 0), right_of(v, 0))
            for i in range(p + 2, 16):
                groups[i] = jnp.where(inside, 0.0, groups[i]) - product[8 * i:8 * i + 8, :]
        if has_next:
            groups[p + 1] = next_group
        hook(p)
    return jnp.concatenate(done, axis=0)


def factor_first(d_ref, li_ref):
    lane = lax.broadcasted_iota(jnp.int32, (8, 128), 1)
    sub = lax.broadcasted_iota(jnp.int32, (8, 128), 0)
    row = lax.broadcasted_iota(jnp.int32, (128, 128), 0)
    col = lax.broadcasted_iota(jnp.int32, (128, 128), 1)
    groups = [d_ref[8 * i:8 * i + 8, :] for i in range(16)]
    li_ref[...] = jnp.where(row >= col, factor_block(groups, lane, sub, lambda p: None), 0.0)


def factor_panel(a_ref, d_ref, xl_ref, xr_ref, li_ref, inv_ref, after):
    n, blocks = PANEL, PANEL // 128
    lane = lax.broadcasted_iota(jnp.int32, (8, 128), 1)
    sub = lax.broadcasted_iota(jnp.int32, (8, 128), 0)
    row = lax.broadcasted_iota(jnp.int32, (128, 128), 0)
    col = lax.broadcasted_iota(jnp.int32, (128, 128), 1)
    wide = lax.broadcasted_iota(jnp.int32, (128, n), 1)
    wide_row = lax.broadcasted_iota(jnp.int32, (128, n), 0)

    def rows_of(k):
        kb = pl.multiple_of(128 * k, 128)
        own = (wide >= kb) & (wide < kb + 128)
        r = jnp.where(own, jnp.where(wide - kb == wide_row, 1.0, 0.0), a_ref[pl.ds(kb, 128), :])
        v = dot6(li_ref[...], r)
        inv_ref[pl.ds(kb, 128), :] = jnp.where(wide < kb + 128, v, 0.0)
        return v

    def next_diagonal(k):
        kb = pl.multiple_of(128 * k, 128)
        nb = pl.multiple_of(128 * jnp.minimum(k + 1, blocks - 1), 128)
        v = parts(dot6(li_ref[...], a_ref[pl.ds(kb, 128), pl.ds(nb, 128)]))
        d_ref[...] = a_ref[pl.ds(nb, 128), pl.ds(nb, 128)] - dot_t(left_of(v, 0), right_of(v, 0))

    next_diagonal(0)

    def turn(k, carry):
        kb = pl.multiple_of(128 * k, 128)
        groups = [d_ref[8 * i:8 * i + 8, :] for i in range(16)]
        prev = k - 1
        pb = pl.multiple_of(128 * prev, 128)
        v = rows_of(prev)
        xl_ref[...] = left_of(parts(v.T), 1)
        xr_ref[...] = right_of(parts(v), 0)

        def hook(p):
            if not 1 <= p <= 8:
                return
            top, first = 128 + 448 * ((p - 1) % 2), 256 * ((p - 1) // 2)
            rows, cols = slice(top, top + 448), slice(first, first + 256)
            below = (top + lax.broadcasted_iota(jnp.int32, (448, 256), 0) >= kb)
            at_col = first + lax.broadcasted_iota(jnp.int32, (448, 256), 1)
            gone = (at_col >= pb) & (at_col < pb + 128)
            old = a_ref[rows, cols]
            new = jnp.where(gone, 0.0, old) - jnp.dot(
                xl_ref[rows, :], xr_ref[:, cols], preferred_element_type=F32
            )
            a_ref[rows, cols] = jnp.where(below, new, old)

        li_ref[...] = jnp.where(row >= col, factor_block(groups, lane, sub, hook), 0.0)
        next_diagonal(k)
        after(k)
        return carry

    lax.fori_loop(1, blocks, turn, 0)
    rows_of(blocks - 1)


def main_kernel(x_ref, gain_ref, damp_ref, hess_ref, fac_ref, upd_ref,
                xs, w, auxs, sx, sz, wn, xn, rms, wide, share, share_in, share_sum, share_y, g,
                slab, other, chip, far, a, d, xl, xr, li, inv, h12, final, extra, h1, hp, hq, u, corner, corner_in, corner_sum, corner_far, ss, rs):
    dp, z, h, x = spot()
    c, y = dp % 2, dp // 2
    column = [at(dp, (z + q // 2) % 4, (h + q % 2) % 2, x) for q in range(1, 8)]
    ring_x = [at(dp, z, h, (x + j) % 4) for j in range(1, 4)]
    ring_z = [at(dp, (z + j) % 4, h, x) for j in range(1, 4)]
    peer_c = at(y * 2 + 1 - c, z, h, x)
    peer_y = at((1 - y) * 2 + c, z, h, x)
    greet_signal(column + ring_x + [peer_c, peer_y])
    sent = []

    def copy(src, dst, i, dev, to=None):
        k = pltpu.make_async_remote_copy(src_ref=src, dst_ref=dst, send_sem=ss.at[i],
                                         recv_sem=rs.at[i if to is None else to],
                                         device_id=dev, device_id_type=MESH)
        return k

    def start(copies):
        for k in copies:
            k.start()
            sent.append(k)

    def arrive(copies):
        for k in copies:
            k.wait_recv()

    part = jnp.zeros((1024, 128), F32)
    for i in range(4):
        v = x_ref[:, 128 * i:128 * i + 128].astype(F32)
        part = part + v * v
    line = jnp.sum(part.T, axis=0, keepdims=True)
    for i in range(8):
        sx[x, i:i + 1, :] = line[:, 128 * i:128 * i + 128]
    is_source = (z == 0) & (h == 0)

    @pl.when(is_source)
    def _():
        own_damp = [v.astype(F32) for v in parts(damp_ref[...])]
        extra_rows = jnp.concatenate([gain_ref[...].astype(F32)] + own_damp + [jnp.zeros((12, 512), F32)], axis=0)
        for q in range(8):
            xs[q, 0:16, :] = extra_rows.astype(BF16)
            xs[q, 16:144, :] = x_ref[128 * q:128 * q + 128, :]
        w[x, 0, 0] = xs[0]

    greet_wait(12)
    sum_x = [copy(sx.at[x], sx.at[x], 47 + j, ring_x[j]) for j in range(3)]
    start(sum_x)

    def scatter(q):
        return [copy(xs.at[q, pl.ds(p, n)], w.at[x, q // 2, q % 2, pl.ds(p, n)], 8 * i + q, column[q - 1], i)
                for i, (p, n) in enumerate([(0, 96), (96, 48)])]

    @pl.when(is_source)
    def _():
        for i in range(2):
            for q in range(1, 8):
                scatter(q)[i].start()

    own = z * 2 + h

    arrive(sum_x)
    sz[own] = (sx[0] + sx[1]) + (sx[2] + sx[3])
    sum_c = [copy(sz.at[own], sz.at[own], 91 + q, column[q - 1]) for q in range(1, 8)]
    start(sum_c)

    own_a, own_b = w.at[x, z, h, pl.ds(0, 96)], w.at[x, z, h, pl.ds(96, 48)]
    step_2b = [copy(own_b, own_b, 26 + q, column[q - 1]) for q in range(1, 8)]
    step_2a = [copy(own_a, own_a, 24 + j, ring_x[j]) for j in range(3)]
    def scattered(p, n, i):
        @pl.when(jnp.logical_not(is_source))
        def _():
            copy(xs.at[0, pl.ds(p, n)], w.at[x, z, h, pl.ds(p, n)], 0, column[0], i).wait_recv()

    scattered(0, 96, 0)
    start(step_2a)
    scattered(96, 48, 1)
    start(step_2b)
    all_b = w.at[x, :, :, pl.ds(96, 48)]
    over_z, over_h = w.at[:, z, h, pl.ds(16, 48)], w.at[:, z, h, pl.ds(64, 32)]
    then_h, then_z = w.at[:, :, h, pl.ds(16, 48)], w.at[:, z, :, pl.ds(64, 32)]
    peer_h = at(dp, z, 1 - h, x)
    step_3z = [copy(over_z, over_z, 36 + j, ring_z[j]) for j in range(3)]
    step_3h = [copy(over_h, over_h, 39, peer_h)]
    step_4h = [copy(then_h, then_h, 40, peer_h)]
    step_4z = [copy(then_z, then_z, 41 + j, ring_z[j]) for j in range(3)]
    step_3b = [copy(all_b, all_b, 44 + j, ring_x[j]) for j in range(3)]
    arrive(step_2a)
    start(step_3z + step_3h)
    arrive(step_3h)
    start(step_4z)
    arrive(step_2b)
    start(step_3b)
    arrive(step_3z)
    start(step_4h)
    arrive(sum_c)

    total = ((sz[0] + sz[1]) + (sz[2] + sz[3])) + ((sz[4] + sz[5]) + (sz[6] + sz[7]))
    inverse = lax.rsqrt(total / D + 1e-05)
    for i in range(8):
        rms[128 * i:128 * i + 128, :] = jnp.broadcast_to(inverse[i:i + 1, :], (128, 128)).T

    @pl.loop(0, 8)
    def _(i):
        rows = pl.ds(pl.multiple_of(i * 128, 128), 128)
        scale = jnp.concatenate([rms[rows, :]] * 4, axis=1)
        xn[rows, :] = (x_ref[rows, :].astype(F32) * scale * gain_ref[...].astype(F32)).astype(BF16)

    for b in range(4):
        v = w[b, z, h, 0:16, :].astype(F32)
        auxs[b, 0:1, :] = v[0:1, :]
        auxs[b, 1:2, :] = (v[1:2, :] + v[2:3, :]) + v[3:4, :]
    arrive(step_4z + step_4h)
    arrive(step_3b)

    def normalise(blocks):
        @pl.loop(0, 8)
        def _(i):
            rows = pl.ds(pl.multiple_of(i * 128, 128), 128)
            scale = jnp.concatenate([rms[rows, :]] * 4, axis=1)
            for b in blocks:
                wn[b, rows, :] = (w[b, i // 2, i % 2, 16:144, :].astype(F32) * scale * auxs[b, 0:1, :]).astype(BF16)

    s = z * 4 + x
    half = pl.ds(pl.multiple_of((s % 2) * 64, 64), 64)
    panels = [pl.ds(0, 1024), pl.ds(1024, 1024)]
    give, keep = pl.ds(pl.multiple_of(32 * (1 - c), 32), 32), pl.ds(pl.multiple_of(32 * c, 32), 32)

    def share_of(m):
        strip = wn[s // 8, :, pl.ds(pl.multiple_of(((s % 8) // 2) * 128, 128), 128)]
        for b in range(2):
            wide[:, 512 * b:512 * b + 512] = dot_t(strip, wn[2 * m + b]) * (1.0 / TOKENS)
        share[:, panels[m]] = wide[half, :]
        k = copy(share.at[give, panels[m]], share_in.at[:, panels[m]], 54 + 36 * m, peer_c)
        start([k])
        return k

    def slab_rows(b):
        slab[512 * b:512 * b + 512, :] = dot_t(wn[b], xn[...]) * (1.0 / TOKENS)

    normalise((0, 1))
    corner[...] = dot_t(wn[0, :, 0:128], wn[0, :, 0:128]) * (1.0 / TOKENS)
    corner_core = [copy(corner, corner_in, 99, peer_c)]
    start(corner_core)
    core_1 = share_of(0)
    normalise((2, 3))
    core_2 = share_of(1)
    slab_rows(0)
    slab_rows(1)
    spans = [(512 * (1 - c), 0, 512), (1024 + 256 * (1 - c), 512, 256), (1536 + 256 * (1 - c), 768, 256)]
    slabs = [
        copy(slab.at[pl.ds(pl.multiple_of(p, 256), n)], other.at[pl.ds(b, n)], 71 + i, peer_c)
        for i, (p, b, n) in enumerate(spans)
    ]
    slab_y = [copy(chip.at[pl.ds(p, 512)], far.at[pl.ds(p, 512)], 73 + i, peer_y)
              for i, p in ((1, 0), (18, 512))]
    start(slabs[:1])
    arrive([core_1])
    share_sum[:, panels[0]] = share[keep, panels[0]] + share_in[:, panels[0]]
    to_y = [copy(share_sum.at[:, panels[0]], share_y.at[:, pl.ds(0, 1024)], 55, peer_y)]
    start(to_y)
    arrive(corner_core)
    corner_sum[...] = corner[...] + corner_in[...]
    corner_y = [copy(corner_sum, corner_far, 100, peer_y)]
    start(corner_y)
    arrive([core_2])
    share_sum[:, panels[1]] = share[keep, panels[1]] + share_in[:, panels[1]]
    far_12 = pl.ds(pl.multiple_of(1024 + 512 * (1 - y), 512), 512)
    near_12 = pl.ds(pl.multiple_of(1024 + 512 * y, 512), 512)
    to_y2 = [copy(share_sum.at[:, far_12], share_y.at[:, pl.ds(1024, 512)], 56, peer_y)]
    start(to_y2)
    arrive(slabs[:1])
    chip[0:512, :] = slab[pl.ds(pl.multiple_of(512 * c, 512), 512), :] + other[0:512, :]
    start(slab_y[:1])
    arrive(to_y)
    g[z, x, c] = share_sum[:, 0:1024] + share_y[:, 0:1024]
    first, second = pl.ds(0, 16), pl.ds(16, 16)

    def gather_1(ref, i):
        one_a, one_b = ref.at[z, x, c, first], ref.at[z, x, c, second]
        return ([copy(one_a, one_a, i + j, ring_x[j]) for j in range(3)],
                [copy(one_b, one_b, i + 3 + j, ring_z[j]) for j in range(3)])

    def gather_2(ref, i):
        row_a, row_b = ref.at[z, :, c, first], ref.at[:, x, c, second]
        return ([copy(row_a, row_a, i + j, ring_z[j]) for j in range(3)],
                [copy(row_b, row_b, i + 3 + j, ring_x[j]) for j in range(3)])

    g1, g2 = gather_1(g, 57), gather_2(g, 63)
    g_core = [copy(g.at[:, :, c, k], g.at[:, :, c, k], i, peer_c) for k, i in ((first, 69), (second, 70))]
    q1, q2 = gather_1(h12, 75), gather_2(h12, 81)
    q_core = [copy(h12.at[:, :, c], h12.at[:, :, c], 87, peer_c)]
    start(g1[0] + g1[1])
    slab_rows(2)
    slab_rows(3)
    start(slabs[1:])
    row = lax.broadcasted_iota(jnp.int32, (128, 128), 0)
    col = lax.broadcasted_iota(jnp.int32, (128, 128), 1)
    arrive(g1[0])
    start(g2[0])
    arrive(g1[1])
    start(g2[1])
    arrive(to_y2)
    h12[z, x, c] = share_sum[:, near_12] + share_y[:, 1024:1536]
    arrive(slabs[1:])
    chip[512:768, :] = slab[pl.ds(pl.multiple_of(1024 + 256 * c, 256), 256), :] + other[512:768, :]
    chip[768:1024, :] = slab[pl.ds(pl.multiple_of(1536 + 256 * c, 256), 256), :] + other[768:1024, :]
    start(slab_y[1:])
    arrive(corner_y)
    d[...] = corner_sum[...] + corner_far[...] + jnp.where(row == col, auxs[0, 1:2, 0:128], 0.0)
    factor_first(d, li)
    arrive(g2[0])
    start(g_core[:1])
    arrive(g2[1])
    start(g_core[1:])
    start(q1[0] + q1[1])
    arrive(g_core)
    for i in range(4):
        for j in range(4):
            for k in range(2):
                lo = 64 * (4 * i + j) + 32 * k
                a[lo:lo + 32, :] = g[i, j, k]
    for k in range(8):
        at_k = slice(128 * k, 128 * k + 128)
        damp = auxs[k // 4, 1:2, 128 * (k % 4):128 * (k % 4) + 128]
        a[at_k, at_k] = a[at_k, at_k] + jnp.where(row == col, damp, 0.0)

    block = pl.multiple_of(512 + 256 * (1 - c), 256)
    to_e = [copy(final.at[pl.ds(0, 512)], extra.at[pl.ds(0, 512)], 88, peer_c),
            copy(final.at[pl.ds(block, 256)], extra.at[pl.ds(512, 256)], 89, peer_c)]

    def after(k):
        @pl.when(k == 1)
        def _():
            arrive(q1[0])
            arrive(q1[1])
            for m in q2[0] + q2[1]:
                m.start()

        @pl.when(k == 4)
        def _():
            arrive(q2[0])
            arrive(q2[1])
            for m in q_core:
                m.start()

        @pl.when(k == 6)
        def _():
            arrive(slab_y)
            final[...] = chip[...] + far[...]
            for m in to_e:
                m.start()

    factor_panel(a, d, xl, xr, li, inv, after)
    arrive(q_core + to_e)

    first_col = (z * 8 + h * 4 + x) * 512
    damp_own = damp_ref[...]

    def damped(value, first_row):
        rows = first_row + lax.broadcasted_iota(jnp.int32, value.shape, 0)
        cols = first_col + lax.broadcasted_iota(jnp.int32, value.shape, 1)
        return value + jnp.where(rows == cols, damp_own, 0.0)

    mine = pl.multiple_of(512 * c, 512)
    theirs = pl.multiple_of(512 * (1 - c), 512)
    h1[pl.ds(mine, 512), :] = damped(final[0:512, :], mine)
    h1[pl.ds(theirs, 512), :] = damped(extra[0:512, :], theirs)

    @pl.when(y == 0)
    def _():
        hess_ref[...] = h1[pl.ds(mine, 512), :]

    @pl.when(y == 1)
    def _():
        p = pl.multiple_of(256 * c, 256)
        q = pl.multiple_of(256 * (1 - c), 256)
        hess_ref[pl.ds(p, 256), :] = damped(final[pl.ds(512 + p, 256), :], 1024 + 512 * c + p)
        hess_ref[pl.ds(q, 256), :] = damped(extra[512:768, :], 1024 + 512 * c + q)

    for i in range(8):
        rows = slice(128 * i, 128 * i + 128)
        hp[rows, 0:512], hq[rows, 0:512] = two_parts(h1[rows, :])
        for j in range(2):
            p = 128 * i + 64 * j
            block12 = jnp.concatenate(
                [h12[i // 2, 2 * (i % 2) + j, m, :, pl.ds(pl.multiple_of(256 * c, 256), 256)] for m in range(2)], axis=0
            )
            hp[p:p + 64, 512:768], hq[p:p + 64, 512:768] = two_parts(block12)
    for i in range(2):
        rows, n = slice(512 * i, 512 * i + 512), 512 * i + 512
        p, q = two_parts(inv[rows, 0:n])
        u[rows, :] = jnp.dot(
            jnp.concatenate([p, p, q], axis=1),
            jnp.concatenate([hp[0:n, :], hq[0:n, :], hp[0:n, :]], axis=0),
            preferred_element_type=F32,
        )
    fac_ref[...] = u[pl.ds(pl.multiple_of(256 * dp, 256), 256), 0:512]
    p, q = two_parts(u[:, 512:768])
    v, r = two_parts(u[:, 0:512])
    upd_ref[...] = damped(
        final[pl.ds(pl.multiple_of(512 + 256 * y, 256), 256), :], 1024 + 256 * dp
    ) - dot_t(jnp.concatenate([p, p, q], axis=0), jnp.concatenate([v, r, v], axis=0))
    for k in sent + q2[0] + q2[1] + q_core + to_e:
        k.wait_send()

    @pl.when(is_source)
    def _():
        for q in range(1, 8):
            for k in scatter(q):
                k.wait_send()


def main(hidden, gain, damping):
    def f32(*shape):
        return pltpu.VMEM(shape, F32)

    def b16(*shape):
        return pltpu.VMEM(shape, BF16)

    return pl.pallas_call(
        main_kernel,
        out_shape=(
            jax.ShapeDtypeStruct((512, 512), F32),
            jax.ShapeDtypeStruct((256, 512), F32),
            jax.ShapeDtypeStruct((256, 512), F32),
        ),
        in_specs=[VM, VM, VM],
        out_specs=(VM, VM, VM),
        scratch_shapes=[
            b16(8, 144, 512), b16(4, 4, 2, 144, 512), f32(4, 8, 512), f32(4, 8, 128), f32(8, 8, 128),
            b16(4, 1024, 512), b16(1024, 512), f32(1024, 128), f32(128, 1024), f32(64, 2048),
            f32(32, 2048), f32(32, 2048), f32(32, 1536), f32(4, 4, 2, 32, 1024),
            f32(2048, 512), f32(1024, 512), f32(1024, 512), f32(1024, 512),
            f32(PANEL, PANEL), f32(128, 128), b16(PANEL, 768), b16(768, PANEL), f32(128, 128),
            f32(PANEL, PANEL), f32(4, 4, 2, 32, 512), f32(1024, 512), f32(768, 512),
            f32(1024, 512), b16(1024, 768), b16(1024, 768), f32(1024, 768),
            f32(128, 128), f32(128, 128), f32(128, 128), f32(128, 128),
            pltpu.SemaphoreType.DMA((101,)),
            pltpu.SemaphoreType.DMA((101,)),
        ],
        compiler_params=params(collective_id=0, has_side_effects=True),
        name="window_panel",
    )(hidden, gain, damping)


def body(hidden_states, norm_gain, damping):
    return main(hidden_states, norm_gain[None], damping[None])


def solution(mesh):
    return jax.shard_map(
        body,
        mesh=mesh,
        in_specs=(P("dp", "mp"), P("mp"), P("mp")),
        out_specs=(P("dp", "mp"), P("dp", "mp"), P("dp", "mp")),
        check_vma=False,
    )
```
